256 devices in a mesh: task: 8 (over z_hi, core), dp: 32 (over z_lo, y, x).
Axes of the slice: x: 4, y: 4, z: 8 (z_hi: 4, z_lo: 2; z = z_hi * 2 + z_lo), core: 2. Of those that a mesh axis runs over, the one named last changes fastest.
Arguments:
- inputs: bfloat16 [32768, 4096], P('dp'), may hold values from -6 to 6
- cotangent: bfloat16 [8, 32768, 1024], P('task', 'dp'), may hold values from -0.22097087 to 0.22097087
- task_order: int32 [8], replicated, may hold values from 0 to 7, each once
- conflict_flags: int32 [8, 8], replicated, may hold values 0 or 1
Outputs:
- combined: bfloat16 [4096, 1024], P(None, 'task')
The draws below stay inside these ranges and needn't reach their ends.
Inputs may be any that keep to these rules, and one draw needn't show every extreme that they name: `task_order`: a permutation of the tasks. `conflict_flags`: diagonal entries are ignored.
All inputs are finite; a program needn't handle non-finite values.
Results may differ from the reference program's by a relative error of at most 0.001.
Values may be sent and summed in bfloat16 or wider, within the bound.
No kernel may reach another device: no remote copies, remote signals or barrier semaphores. Data moves between devices by JAX's collectives and lax.ppermute only.
A program may use at most 128 MiB of HBM per device.

```python
import math
import jax
import jax.numpy as jnp
from jax import lax

D = 4096
KVW = 1024
TASKS = 8
TOKENS = 32768


def latent_factors(key):
    return jax.random.normal(jax.random.fold_in(key, 21), (TOKENS, 32, 16), jnp.float32)


def draw_inputs(key, part):
    latent = latent_factors(key)
    loading = jax.random.normal(jax.random.fold_in(key, 22), (16, 32, D // 32), jnp.float32) / 4.0
    independent = jax.random.normal(jax.random.fold_in(key, 23), (TOKENS, D), jnp.float32)
    grouped = jnp.einsum('ngr,rgf->ngf', latent, loading).reshape(TOKENS, D)
    values = 0.8 * grouped + 0.6 * independent
    position = jnp.arange(D, dtype=jnp.float32) / (D - 1.0)
    low_end = math.log(0.5)
    high_end = math.log(2.0)
    feature_scale = jnp.exp(low_end + (high_end - low_end) * position)
    values = values * feature_scale[None, :]
    return jnp.clip(values, -6.0, 6.0).astype(jnp.bfloat16)


def draw_cotangent(key, part):
    key_mix = jax.random.fold_in(key, 11)
    key_base = jax.random.fold_in(key, 12)
    key_own = jax.random.fold_in(key, 13)
    key_basis = jax.random.fold_in(key, 15)
    key_signs = jax.random.fold_in(key, 16)
    key_columns = jax.random.fold_in(key, 17)
    key_order = jax.random.fold_in(key, 18)
    key_second = jax.random.fold_in(key, 19)
    key_other = jax.random.fold_in(key, 20)
    sign_values = jnp.where(jax.random.bernoulli(key_order, 0.5, (TASKS,)), 1.0, -1.0).astype(jnp.float32)
    magnitude = jax.random.uniform(key_mix, (TASKS,), jnp.float32, 0.3, 1.0)
    mixing = (sign_values * magnitude)[:, None, None]
    second_mix = jax.random.uniform(key_second, (TASKS, 1, 1), jnp.float32, -1.0, 1.0)
    latent = latent_factors(key)
    basis_rows = jax.random.normal(key_basis, (512, KVW), jnp.float32)
    row_signs = jax.random.uniform(key_signs, (TASKS, 32), jnp.float32, -1.0, 1.0)
    column_scales = jnp.exp(jax.random.uniform(key_columns, (TASKS, 8), jnp.float32, math.log(0.5), math.log(2.0)))
    weighted = (latent[None] * row_signs[:, None, :, None]).reshape(TASKS, TOKENS, 512)
    structured = jnp.einsum('tnk,kc->tnc', weighted, basis_rows)
    structured = structured * jnp.repeat(column_scales, KVW // 8, axis=1)[:, None, :]
    structured = structured * (0.25 / math.sqrt(512.0))
    shared = jnp.clip(jax.random.normal(key_base, (TOKENS, KVW), jnp.float32), -4.0, 4.0)
    other = jnp.clip(jax.random.normal(key_other, (TOKENS, KVW), jnp.float32), -4.0, 4.0)
    private = jnp.clip(jax.random.normal(key_own, (TASKS, TOKENS, KVW), jnp.float32), -4.0, 4.0)
    raw = 0.8 * mixing * shared[None] + second_mix * other[None] + 0.45 * private + structured
    raw = jnp.clip(raw, -4.0, 4.0)
    values = raw / math.sqrt(TOKENS)
    return values.astype(jnp.bfloat16)


def set_ends(values, key, smallest, high):
    index_at = [jax.random.randint(jax.random.fold_in(key, axis), (), 0, length) for axis, length in enumerate(values.shape)]
    main_axis = values.shape.index(max(values.shape))
    beside = index_at[:main_axis] + [(index_at[main_axis] + 1) % values.shape[main_axis]] + index_at[main_axis + 1:]
    return values.at[tuple(index_at)].set(smallest).at[tuple(beside)].set(high)


def setup_inputs(seed: int = 0) -> dict:
    key_of = jax.random.split(jax.random.key(seed), 5)
    inputs = draw_inputs(jax.random.fold_in(key_of[4], 71), 0)
    cotangent = draw_cotangent(jax.random.fold_in(key_of[4], 71), 0)
    task_order = jax.random.permutation(key_of[2], TASKS).astype(jnp.int32)
    conflict_flags = set_ends((jax.random.randint(key_of[3], (TASKS, TASKS), 0, 4) < 3).astype(jnp.int32), jax.random.fold_in(key_of[3], 1), 0, 1)
    return {"inputs": inputs, "cotangent": cotangent, "task_order": task_order, "conflict_flags": conflict_flags}


def project_weights(gram_matrix, task_order, conflict_flags):
    count = gram_matrix.shape[0]
    labels = jnp.arange(count, dtype=jnp.int32)
    coefficients = jnp.eye(count, dtype=jnp.float32)
    for position in range(count):
        target = task_order[position]
        pick_column = (labels == target).astype(jnp.float32)
        column = jnp.dot(gram_matrix, pick_column, precision=lax.Precision.HIGHEST)
        inner_dots = jnp.dot(coefficients, column, precision=lax.Precision.HIGHEST)
        own_square = jnp.sum(pick_column * column)
        active = jnp.dot(conflict_flags.astype(jnp.float32), pick_column, precision=lax.Precision.HIGHEST) * (1.0 - pick_column)
        removed = jnp.minimum(inner_dots, 0.0) / own_square * active
        coefficients = coefficients - removed[:, None] * pick_column[None, :]
    return jnp.sum(coefficients, axis=0)


def reference(inputs, cotangent, task_order, conflict_flags):
    def one_task(task_cot):
        return lax.dot_general(inputs, task_cot, (((0,), (0,)), ((), ())), preferred_element_type=jnp.float32)

    grads = lax.map(one_task, cotangent)
    gram_matrix = jnp.einsum("tab,sab->ts", grads, grads, precision=lax.Precision.HIGHEST)
    weights = project_weights(gram_matrix, task_order, conflict_flags)
    combined = jnp.einsum("t,tab->ab", weights, grads, precision=lax.Precision.HIGHEST)
    return combined.astype(jnp.bfloat16)
```

```python
import itertools

import jax
import jax.numpy as jnp
import numpy as np
from jax import lax
from jax.experimental import pallas as pl
from jax.experimental.pallas import tpu as pltpu
from jax.sharding import Mesh
from jax.sharding import PartitionSpec as P

AXES = ("zh", "core", "zl", "y", "x")
SIZES = (4, 2, 2, 4, 4)
DP = ("zl", "y", "x")
TASK = ("zh", "core")
F32, BF16, I16, I32 = jnp.float32, jnp.bfloat16, jnp.int16, jnp.int32

PARTNER = {"a": (1, 0, 3, 2), "b": (3, 2, 1, 0)}
BIT = {"a": (0, 1, 1, 0), "b": (0, 0, 1, 1)}
ORDER = {
    (0, 0): ("xa", "ya", "xb", "yb", "z"),
    (0, 1): ("xb", "yb", "xa", "ya", "z"),
    (1, 0): ("ya", "xa", "yb", "xb", "z"),
    (1, 1): ("yb", "xb", "ya", "xa", "z"),
}
FULL = 32000.0
STEPS = 64.0
EXTRA = 16


def coordinates():
    return [dict(zip(AXES, v)) for v in itertools.product(*map(range, SIZES))]


def linear(co):
    index = 0
    for axis, size in zip(AXES, SIZES):
        index = index * size + co[axis]
    return index


def bit_of(co, dim):
    return co["zl"] if dim == "z" else BIT[dim[1]][co[dim[0]]]


def partner(co, dim):
    if dim == "z":
        return {**co, "zl": 1 - co["zl"]}
    return {**co, dim[0]: PARTNER[dim[1]][co[dim[0]]]}


def swap_along(value, dims):
    pairs = [(linear(co), linear(partner(co, dims[co["core"]]))) for co in coordinates()]
    return lax.ppermute(value, AXES, pairs)


def position(co, core, chunk):
    place = 0
    for dim in ORDER[core, chunk]:
        place = 2 * place + bit_of(co, dim)
    return place


def device_table():
    rows = []
    for co in coordinates():
        core = co["core"]
        row = [core, co["zh"]]
        for chunk in range(2):
            bits = [bit_of(co, dim) for dim in ORDER[core, chunk]]
            base = 4 * core + 2 * chunk
            row += [base + 1 - bits[0], base + bits[0]] + bits[1:]
        rows.append(row + [0] * (16 - len(row)))
    return np.asarray(rows, np.int32)


def encode(tile):
    top = jnp.maximum(jnp.max(jnp.abs(tile), axis=0, keepdims=True), 1e-30)
    code = jnp.ceil(jnp.log(top) * STEPS)
    values = jnp.round(tile * (jnp.exp(code * (-1.0 / STEPS)) * FULL))
    return values.astype(I32).astype(I16), code


def scales(codes):
    return jnp.exp(codes.astype(I32).astype(F32) * (1.0 / STEPS)) * (1.0 / FULL)


def floats(values):
    return values.astype(I32).astype(F32)


def params(mib=40):
    return pltpu.CompilerParams(vmem_limit_bytes=mib << 20)


def call(kernel, scalars, grid, inputs, in_specs, out_shape, out_specs, scratch, flops, nbytes, **extra):
    return pl.pallas_call(
        kernel,
        out_shape=out_shape,
        grid_spec=pltpu.PrefetchScalarGridSpec(
            num_scalar_prefetch=1,
            grid=grid,
            in_specs=in_specs,
            out_specs=out_specs,
            scratch_shapes=scratch,
        ),
        compiler_params=params(),
        cost_estimate=pl.CostEstimate(flops=flops, bytes_accessed=nbytes, transcendentals=0),
        **extra,
    )(scalars, *inputs)


def whole(shape):
    return pl.BlockSpec(shape, lambda *_: (0,) * len(shape))


ROWS = 512
TILE = 128
COLS = 256


def dot_rows(transposed, cot):
    return lax.dot_general(transposed, cot, (((1,), (0,)), ((), ())), preferred_element_type=F32)


def send_kernel(s_ref, x_ref, own_ref, other_ref, out_ref, turned, codes):
    step = pl.program_id(0)

    @pl.when(step == 0)
    def _():
        turned[...] = x_ref[...].T
        codes[...] = jnp.zeros_like(codes)

    column = pl.ds(pl.multiple_of(lax.rem(step, 4) * COLS, COLS), COLS)

    def one(task, cot_ref):
        product = dot_rows(turned[...], cot_ref[...])
        for tile in range(ROWS // TILE):
            values, code = encode(product[tile * TILE : (tile + 1) * TILE])
            out_ref[pl.ds(task * ROWS + tile * TILE, TILE), column] = values
            codes[pl.ds(task * (ROWS // TILE) + tile, 1), column] = code

    @pl.when(step < 4)
    def _():
        one(0, own_ref)

    @pl.when(step >= 4)
    def _():
        one(1, other_ref)

    @pl.when(step == 7)
    def _():
        out_ref[2 * ROWS :, :] = codes[...].astype(I32).astype(I16)


def cot_specs(tokens):
    return [
        pl.BlockSpec((tokens, COLS), lambda n, s: (0, jnp.minimum(n, 3))),
        pl.BlockSpec((tokens, COLS), lambda n, s: (0, jnp.maximum(n - 4, 0))),
    ]


def send_term(table, slot, inputs, own, other):
    tokens, width = own.shape
    return call(
        send_kernel,
        table,
        (8,),
        (inputs, own, other),
        [pl.BlockSpec((tokens, ROWS), lambda n, s: (0, s[slot]))] + cot_specs(tokens),
        jax.ShapeDtypeStruct((2 * ROWS + EXTRA, width), I16),
        whole((2 * ROWS + EXTRA, width)),
        [pltpu.VMEM((ROWS, tokens), BF16), pltpu.VMEM((EXTRA, width), F32)],
        4 * ROWS * tokens * width,
        7 << 20,
    )


def keep_kernel(s_ref, x_ref, own_ref, other_ref, out_ref, turned):
    step = pl.program_id(0)

    @pl.when(step == 0)
    def _():
        turned[...] = x_ref[...].T

    @pl.when(step < 4)
    def _():
        out_ref[0] = dot_rows(turned[...], own_ref[...])

    @pl.when(step >= 4)
    def _():
        out_ref[0] = dot_rows(turned[...], other_ref[...])


def keep_term(table, slot, inputs, own, other):
    tokens, width = own.shape
    return call(
        keep_kernel,
        table,
        (8,),
        (inputs, own, other),
        [pl.BlockSpec((tokens, ROWS), lambda n, s: (0, s[slot]))] + cot_specs(tokens),
        jax.ShapeDtypeStruct((2, ROWS, width), F32),
        pl.BlockSpec((1, ROWS, COLS), lambda n, s: (n // 4, 0, lax.rem(n, 4))),
        [pltpu.VMEM((ROWS, tokens), BF16)],
        4 * ROWS * tokens * width,
        9 << 20,
    )


def level(table, slot, kept, arrived):
    _, rows, width = kept.shape
    half = rows // 2
    tile = min(TILE, half)
    per = half // tile
    code_rows = min(TILE, rows)

    def kernel(s_ref, keep_ref, give_ref, keep_in, give_in, codes_ref, sum_ref, out_ref, scale, codes):
        task, j = pl.program_id(0), pl.program_id(1)
        bit = s_ref[slot]

        @pl.when((task == 0) & (j == 0))
        def _():
            scale[...] = scales(codes_ref[...])
            codes[...] = jnp.zeros_like(codes)

        def row_of(side):
            return (task * rows + side * half + j * tile) // code_rows

        sum_ref[0] = keep_ref[0] + floats(keep_in[...]) * scale[pl.ds(row_of(bit), 1), :]
        give = give_ref[0] + floats(give_in[...]) * scale[pl.ds(row_of(1 - bit), 1), :]
        values, code = encode(give)
        at = task * per + j
        out_ref[pl.ds(pl.multiple_of(at * tile, tile), tile), :] = values
        codes[pl.ds(at, 1), :] = code

        @pl.when((task == 1) & (j == per - 1))
        def _():
            out_ref[2 * half :, :] = codes[...].astype(I32).astype(I16)

    return call(
        kernel,
        table,
        (2, per),
        (kept, kept, arrived, arrived, arrived),
        [
            pl.BlockSpec((1, tile, width), lambda t, j, s: (t, s[slot] * per + j, 0)),
            pl.BlockSpec((1, tile, width), lambda t, j, s: (t, (1 - s[slot]) * per + j, 0)),
            pl.BlockSpec((tile, width), lambda t, j, s: ((2 * t + s[slot]) * per + j, 0)),
            pl.BlockSpec((tile, width), lambda t, j, s: ((2 * t + 1 - s[slot]) * per + j, 0)),
            pl.BlockSpec((EXTRA, width), lambda t, j, s: (2 * rows // EXTRA, 0)),
        ],
        (jax.ShapeDtypeStruct((2, half, width), F32), jax.ShapeDtypeStruct((2 * half + EXTRA, width), I16)),
        (pl.BlockSpec((1, tile, width), lambda t, j, s: (t, j, 0)), whole((2 * half + EXTRA, width))),
        [pltpu.VMEM((EXTRA, width), F32), pltpu.VMEM((EXTRA, width), F32)],
        16 * rows * width,
        2 * rows * width * 9,
    )


def join_level(table, slot, kept, arrived):
    _, rows, width = kept[0].shape
    half = rows // 2

    def kernel(s_ref, keep_a, keep_b, in_a, in_b, sum_ref, out_ref):
        bit = s_ref[slot]
        out_codes = []
        for chunk, (keep, arr) in enumerate(((keep_a, in_a), (keep_b, in_b))):
            scale = scales(arr[2 * rows :, :])
            for task in range(2):

                def part(side):
                    at = pl.multiple_of(side * half, half)
                    values = floats(arr[pl.ds(pl.multiple_of(task * rows + side * half, half), half), :])
                    return keep[task, pl.ds(at, half), :] + values * scale[task : task + 1]

                sum_ref[chunk, task] = part(bit)
                values, code = encode(part(1 - bit))
                n = 2 * chunk + task
                out_ref[n * half : (n + 1) * half, :] = values
                out_codes.append(code)
        out_codes.append(jnp.zeros((EXTRA - 4, width), F32))
        out_ref[4 * half :, :] = jnp.concatenate(out_codes, axis=0).astype(I32).astype(I16)

    shapes = ((2, rows, width), (2, rows, width), (2 * rows + EXTRA, width), (2 * rows + EXTRA, width))
    return call(
        kernel,
        table,
        (1,),
        (*kept, *arrived),
        [whole(s) for s in shapes],
        (jax.ShapeDtypeStruct((2, 2, half, width), F32), jax.ShapeDtypeStruct((4 * half + EXTRA, width), I16)),
        (whole((2, 2, half, width)), whole((4 * half + EXTRA, width))),
        [],
        32 * rows * width,
        4 * rows * width * 9,
    )


def columns_kernel(s_ref, keep_ref, in_ref, own_ref, out1, out2, out3, total):
    zh = s_ref[1]
    rows = keep_ref.shape[2]
    scale = scales(in_ref[4 * rows :, :])
    for n in range(4):
        total[n * rows : (n + 1) * rows, :] = keep_ref[n // 2, n % 2] + floats(
            in_ref[n * rows : (n + 1) * rows, :]
        ) * scale[n : n + 1]
    wide = own_ref.shape[1]

    def block(k):
        return total[:, pl.ds(pl.multiple_of(lax.rem(zh + k, 4) * wide, wide), wide)]

    own_ref[...] = block(0)
    for k, out in ((1, out1), (2, out2), (3, out3)):
        value = block(k)
        codes = []
        for n in range(4):
            values, code = encode(value[n * rows : (n + 1) * rows])
            out[n * rows : (n + 1) * rows, :] = values
            codes.append(code)
        codes.append(jnp.zeros((EXTRA - 4, wide), F32))
        out[4 * rows :, :] = jnp.concatenate(codes, axis=0).astype(I32).astype(I16)


def columns(table, kept, arrived):
    rows, width = kept.shape[2:]
    wide = width // 4
    coded = (4 * rows + EXTRA, wide)
    return call(
        columns_kernel,
        table,
        (1,),
        (kept, arrived),
        [whole(kept.shape), whole(arrived.shape)],
        (jax.ShapeDtypeStruct((4 * rows, wide), F32),) + (jax.ShapeDtypeStruct(coded, I16),) * 3,
        (whole((4 * rows, wide)),) + (whole(coded),) * 3,
        [pltpu.VMEM((4 * rows, width), F32)],
        16 * rows * width,
        8 * rows * width * 4,
    )


def lanes(shape, dim):
    return lax.broadcasted_iota(I32, shape, dim)


def gram_kernel(s_ref, own_ref, in1, in2, in3, grads_ref, gram_ref):
    core, zh = s_ref[0], s_ref[1]
    rows = own_ref.shape[0] // 4

    def place(k, tiles):
        pair = lax.rem(zh + 4 - k, 4)
        for n in range(4):
            chunk, task = n // 2, n % 2
            mine = 2 * pair + (task + core - 2 * task * core)
            grads_ref[mine, chunk * rows : (chunk + 1) * rows, :] = tiles(n)

    place(0, lambda n: own_ref[n * rows : (n + 1) * rows, :])
    for k, ref in ((1, in1), (2, in2), (3, in3)):
        scale = scales(ref[4 * rows :, :])
        place(k, lambda n: floats(ref[n * rows : (n + 1) * rows, :]) * scale[n : n + 1])

    grads = [grads_ref[t] for t in range(8)]
    lane, sub = lanes((8, 128), 1), lanes((8, 128), 0)
    matrix = jnp.zeros((8, 128), F32)
    for s in range(8):
        for t in range(s, 8):
            product = grads[s] * grads[t]
            folded = product[:, :128] + product[:, 128:]
            total = jnp.sum(jnp.sum(folded, axis=0, keepdims=True), axis=1, keepdims=True)
            here = ((sub == s) & (lane == t)) | ((sub == t) & (lane == s))
            matrix = jnp.where(here, total, matrix)
    line = jnp.zeros((8, 128), F32)
    for s in range(8):
        row = jnp.where(sub == s, matrix, 0.0)
        line = line + (row if s == 0 else pltpu.roll(row, 8 * s, 1))
    flat = jnp.sum(line, axis=0, keepdims=True)
    gram_ref[...] = jnp.broadcast_to(flat, gram_ref.shape)


def gram(table, own, arrived):
    rows, wide = own.shape
    coded = arrived[0].shape
    return call(
        gram_kernel,
        table,
        (1,),
        (own, *arrived),
        [whole(own.shape)] + [whole(coded)] * 3,
        (jax.ShapeDtypeStruct((8, rows // 2, wide), F32), jax.ShapeDtypeStruct((256, 128), F32)),
        (whole((8, rows // 2, wide)), whole((256, 128))),
        [],
        80 * rows * wide,
        16 * rows * wide,
    )


def combine_kernel(s_ref, order_ref, flags_ref, gram_ref, grads_ref, mine_ref, give_ref):
    core = s_ref[0]
    lane, sub = lanes((8, 128), 1), lanes((8, 128), 0)
    flat = jnp.broadcast_to(jnp.sum(gram_ref[...], axis=0, keepdims=True), (8, 128))
    matrix = jnp.zeros((8, 128), F32)
    for s in range(8):
        row = flat if s == 0 else pltpu.roll(flat, 128 - 8 * s, 1)
        matrix = jnp.where((sub == s) & (lane < 8), row, matrix)
    flags = flags_ref[...].astype(F32)
    small = lanes((8, 8), 1)
    coefficients = jnp.where(lane == sub, 1.0, 0.0)
    for k in range(8):
        target = order_ref[k]
        row = jnp.sum(jnp.where(sub == target, matrix, 0.0), axis=0, keepdims=True)
        dots = jnp.sum(coefficients * row, axis=1, keepdims=True)
        square = jnp.sum(jnp.where(lane[:1] == target, row, 0.0), axis=1, keepdims=True)
        active = jnp.sum(jnp.where(small == target, flags, 0.0), axis=1, keepdims=True)
        active = jnp.where(sub[:, :1] == target, 0.0, active)
        removed = jnp.minimum(dots, 0.0) / square * active
        coefficients = coefficients - jnp.where(lane == target, removed, 0.0)
    weights = jnp.sum(coefficients, axis=0, keepdims=True)
    total = None
    for t in range(8):
        weight = jnp.sum(jnp.where(lane[:1] == t, weights, 0.0), axis=1, keepdims=True)
        term = weight * grads_ref[t]
        total = term if total is None else total + term
    left, right = total[:, :128].astype(BF16), total[:, 128:].astype(BF16)

    @pl.when(core == 0)
    def _():
        mine_ref[...] = left
        give_ref[...] = right

    @pl.when(core == 1)
    def _():
        mine_ref[...] = right
        give_ref[...] = left


def combine(table, order, flags, grams, grads):
    rows = grads.shape[1]
    part = jax.ShapeDtypeStruct((rows, 128), BF16)
    return call(
        combine_kernel,
        table,
        (1,),
        (order, flags, grams, grads),
        [pl.BlockSpec(memory_space=pltpu.SMEM), whole((8, 8)), whole((256, 128)), whole(grads.shape)],
        (part, part),
        (whole((rows, 128)),) * 2,
        [],
        20 * rows * 256,
        40 * rows * 256,
    )


def place_kernel(in_ref, out_ref):
    rows = in_ref.shape[1] // 4
    for index, (zl, y, x) in enumerate(itertools.product(range(2), range(4), range(4))):
        co = {"zl": zl, "y": y, "x": x}
        for n in range(4):
            at = (n * 32 + position(co, n // 2, n % 2)) * rows
            out_ref[at : at + rows, :] = in_ref[index, n * rows : (n + 1) * rows, :]


def place(gathered):
    count, rows, cols = gathered.shape
    return pl.pallas_call(
        place_kernel,
        out_shape=jax.ShapeDtypeStruct((count * rows, cols), BF16),
        compiler_params=params(),
        cost_estimate=pl.CostEstimate(flops=0, bytes_accessed=4 * count * rows * cols, transcendentals=0),
    )(gathered)


def on_device(inputs, cotangent, task_order, conflict_flags):
    table = jnp.asarray(device_table())[lax.axis_index(AXES)]
    core = lax.axis_index("core")
    own = cotangent[0]
    other = lax.ppermute(own, "core", [(0, 1), (1, 0)])

    dims = [[(ORDER[0, chunk][n], ORDER[1, chunk][n]) for n in range(5)] for chunk in range(2)]
    slots = [2, 8]
    arrived, kept = [], []
    for chunk in range(2):
        coded = send_term(table, slots[chunk], inputs, own, other)
        arrived.append(swap_along(coded, dims[chunk][0]))
    for chunk in range(2):
        kept.append(keep_term(table, slots[chunk] + 1, inputs, own, other))
    for n in range(1, 4):
        for chunk in range(2):
            kept[chunk], coded = level(table, slots[chunk] + 1 + n, kept[chunk], arrived[chunk])
            arrived[chunk] = swap_along(coded, dims[chunk][n])
    summed, coded = join_level(table, slots[0] + 5, kept, arrived)
    own_cols, *coded = columns(table, summed, swap_along(coded, ("z", "z")))
    turned = [
        lax.ppermute(value, "zh", [(i, (i + k) % 4) for i in range(4)]) for k, value in zip((1, 2, 3), coded)
    ]
    grads, grams = gram(table, own_cols, turned)
    grams = lax.all_to_all(grams, AXES, split_axis=0, concat_axis=0, tiled=True)
    mine, give = combine(table, task_order, conflict_flags, grams, grads)
    taken = lax.ppermute(give, "core", [(0, 1), (1, 0)])
    first = jnp.where(core == 0, mine, taken)
    second = jnp.where(core == 0, taken, mine)
    block = jnp.concatenate([first, second], axis=0)
    copies = jnp.broadcast_to(block, (32, *block.shape))
    gathered = lax.all_to_all(copies, DP, split_axis=0, concat_axis=0, tiled=True)
    return place(gathered)


def solution(mesh):
    split = Mesh(mesh.devices.reshape(SIZES), AXES)
    placed = (P(DP, None), P(TASK, DP, None), P(), P())
    return jax.shard_map(
        on_device, mesh=split, in_specs=placed, out_specs=P(None, TASK), check_vma=False
    )
```

```python
import itertools

import jax
import jax.numpy as jnp
import numpy as np
from jax import lax
from jax.experimental import pallas as pl
from jax.experimental.pallas import tpu as pltpu
from jax.sharding import Mesh
from jax.sharding import PartitionSpec as P

AXES = ("zh", "core", "zl", "y", "x")
SIZES = (4, 2, 2, 4, 4)
DP = ("zl", "y", "x")
TASK = ("zh", "core")
F32, BF16, I16, I32 = jnp.float32, jnp.bfloat16, jnp.int16, jnp.int32

PARTNER = {"a": (1, 0, 3, 2), "b": (3, 2, 1, 0)}
BIT = {"a": (0, 1, 1, 0), "b": (0, 0, 1, 1)}
ORDER = {
    (0, 0): ("xa", "yb", "xb", "ya", "z"),
    (0, 1): ("yb", "xa", "ya", "xb", "z"),
    (1, 0): ("ya", "xb", "xa", "yb", "z"),
    (1, 1): ("xb", "ya", "yb", "xa", "z"),
}
FULL = 32000.0
STEPS = 64.0
EXTRA = 16


def coordinates():
    return [dict(zip(AXES, v)) for v in itertools.product(*map(range, SIZES))]


def linear(co):
    index = 0
    for axis, size in zip(AXES, SIZES):
        index = index * size + co[axis]
    return index


def bit_of(co, dim):
    return co["zl"] if dim == "z" else BIT[dim[1]][co[dim[0]]]


def partner(co, dim):
    if dim == "z":
        return {**co, "zl": 1 - co["zl"]}
    return {**co, dim[0]: PARTNER[dim[1]][co[dim[0]]]}


def swap_along(value, dims):
    pairs = [(linear(co), linear(partner(co, dims[co["core"]]))) for co in coordinates()]
    return lax.ppermute(value, AXES, pairs)


def position(co, core, chunk):
    place = 0
    for dim in ORDER[core, chunk]:
        place = 2 * place + bit_of(co, dim)
    return place


def device_table():
    rows = []
    for co in coordinates():
        core = co["core"]
        row = [core, co["zh"]]
        for chunk in range(2):
            bits = [bit_of(co, dim) for dim in ORDER[core, chunk]]
            row += bits + [0]
        rows.append(row + [0] * (16 - len(row)))
    return np.asarray(rows, np.int32)


def encode(tile):
    top = jnp.maximum(jnp.max(jnp.abs(tile), axis=0, keepdims=True), 1e-30)
    code = jnp.ceil(jnp.log(top) * STEPS)
    values = jnp.round(tile * (jnp.exp(code * (-1.0 / STEPS)) * FULL))
    return values.astype(I32).astype(I16), code


def scales(codes):
    return jnp.exp(codes.astype(I32).astype(F32) * (1.0 / STEPS)) * (1.0 / FULL)


def floats(values):
    return values.astype(I32).astype(F32)


def params(mib=14):
    return pltpu.CompilerParams(vmem_limit_bytes=mib << 20)


def call(kernel, scalars, grid, inputs, in_specs, out_shape, out_specs, scratch, flops, nbytes, **extra):
    return pl.pallas_call(
        kernel,
        out_shape=out_shape,
        grid_spec=pltpu.PrefetchScalarGridSpec(
            num_scalar_prefetch=1,
            grid=grid,
            in_specs=in_specs,
            out_specs=out_specs,
            scratch_shapes=scratch,
        ),
        compiler_params=params(),
        cost_estimate=pl.CostEstimate(flops=flops, bytes_accessed=nbytes, transcendentals=0),
        **extra,
    )(scalars, *inputs)


def whole(shape):
    return pl.BlockSpec(shape, lambda *_: (0,) * len(shape))


ROWS = 512
TILE = 128


def encode_kernel(s_ref, term_ref, out_ref, codes):
    tile = pl.program_id(0)
    values, code = encode(term_ref[...])
    out_ref[pl.ds(pl.multiple_of(tile * TILE, TILE), TILE), :] = values
    codes[pl.ds(tile, 1), :] = code

    @pl.when(tile == ROWS // TILE - 1)
    def _():
        out_ref[ROWS:, :] = codes[...].astype(I32).astype(I16)


def encode_term(table, slot, term):
    rows, width = ROWS, term.shape[1]
    per = rows // TILE
    return call(
        encode_kernel,
        table,
        (per,),
        (term,),
        [pl.BlockSpec((TILE, width), lambda n, s: ((1 - s[slot]) * per + n, 0))],
        jax.ShapeDtypeStruct((rows + EXTRA, width), I16),
        whole((rows + EXTRA, width)),
        [pltpu.VMEM((EXTRA, width), F32)],
        8 * rows * width,
        6 * rows * width,
    )


def term_of(inputs, start, cot):
    part = lax.dynamic_slice(inputs, (0, start), (inputs.shape[0], 2 * ROWS))
    return lax.dot_general(part, cot, (((0,), (0,)), ((), ())), preferred_element_type=F32)


def after(value, *others):
    return lax.optimization_barrier((value, *others))[0]


def level(table, slot, kept, arrived, first=None):
    tasks, rows, width = kept.shape
    rows = rows if first is None else rows // 2
    half = rows // 2
    tile = min(TILE, half)
    per = half // tile
    code_rows = min(TILE, rows)

    def skip(s):
        return 0 if first is None else s[first] * 2 * per

    def kernel(s_ref, keep_ref, give_ref, keep_in, give_in, codes_ref, sum_ref, out_ref, scale, codes):
        task, j = pl.program_id(0), pl.program_id(1)
        bit = s_ref[slot]

        @pl.when((task == 0) & (j == 0))
        def _():
            scale[...] = scales(codes_ref[...])
            codes[...] = jnp.zeros_like(codes)

        def row_of(side):
            return (task * rows + side * half + j * tile) // code_rows

        give = give_ref[0] + floats(give_in[...]) * scale[pl.ds(row_of(1 - bit), 1), :]
        values, code = encode(give)
        at = task * per + j
        out_ref[pl.ds(pl.multiple_of(at * tile, tile), tile), :] = values
        codes[pl.ds(at, 1), :] = code
        sum_ref[0] = keep_ref[0] + floats(keep_in[...]) * scale[pl.ds(row_of(bit), 1), :]

        @pl.when((task == tasks - 1) & (j == per - 1))
        def _():
            out_ref[tasks * half :, :] = codes[...].astype(I32).astype(I16)

    return call(
        kernel,
        table,
        (tasks, per),
        (kept, kept, arrived, arrived, arrived),
        [
            pl.BlockSpec((1, tile, width), lambda t, j, s: (t, skip(s) + s[slot] * per + j, 0)),
            pl.BlockSpec((1, tile, width), lambda t, j, s: (t, skip(s) + (1 - s[slot]) * per + j, 0)),
            pl.BlockSpec((tile, width), lambda t, j, s: ((2 * t + s[slot]) * per + j, 0)),
            pl.BlockSpec((tile, width), lambda t, j, s: ((2 * t + 1 - s[slot]) * per + j, 0)),
            pl.BlockSpec((EXTRA, width), lambda t, j, s: (tasks * rows // EXTRA, 0)),
        ],
        (
            jax.ShapeDtypeStruct((tasks, half, width), F32),
            jax.ShapeDtypeStruct((tasks * half + EXTRA, width), I16),
        ),
        (pl.BlockSpec((1, tile, width), lambda t, j, s: (t, j, 0)), whole((tasks * half + EXTRA, width))),
        [pltpu.VMEM((EXTRA, width), F32), pltpu.VMEM((EXTRA, width), F32)],
        8 * tasks * rows * width,
        tasks * rows * width * 9,
    )


def join_tasks(table, slot, kept, arrived):
    _, rows, width = kept[0].shape
    half = rows // 2

    def kernel(s_ref, keep_a, keep_b, in_a, in_b, sum_ref, out_ref, scale):
        bit = s_ref[slot]
        out_codes = []
        for task, (keep, arr) in enumerate(((keep_a, in_a), (keep_b, in_b))):
            scale[...] = scales(arr[rows:, :])

            def part(side):
                at = pl.ds(pl.multiple_of(side * half, half), half)
                return keep[0, at, :] + floats(arr[at, :]) * scale[pl.ds(side * half // TILE, 1), :]

            values, code = encode(part(1 - bit))
            out_ref[task * half : (task + 1) * half, :] = values
            out_codes.append(code)
            sum_ref[task] = part(bit)
        out_codes.append(jnp.zeros((EXTRA - 2, width), F32))
        out_ref[2 * half :, :] = jnp.concatenate(out_codes, axis=0).astype(I32).astype(I16)

    shapes = ((1, rows, width), (1, rows, width), (rows + EXTRA, width), (rows + EXTRA, width))
    return call(
        kernel,
        table,
        (1,),
        (*kept, *arrived),
        [whole(s) for s in shapes],
        (jax.ShapeDtypeStruct((2, half, width), F32), jax.ShapeDtypeStruct((2 * half + EXTRA, width), I16)),
        (whole((2, half, width)), whole((2 * half + EXTRA, width))),
        [pltpu.VMEM((EXTRA, width), F32)],
        16 * rows * width,
        2 * rows * width * 9,
    )


def line_blocks(kept, arrived):
    _, rows, width = kept[0].shape
    half, wide = rows // 2, width // 4

    def kernel(keep_a, keep_b, in_a, in_b, out_ref, total):
        for chunk, (keep, arr) in enumerate(((keep_a, in_a), (keep_b, in_b))):
            scale = scales(arr[2 * rows :, :])
            for task in range(2):
                values = floats(arr[task * rows : (task + 1) * rows, :])
                total[2 * chunk + task] = keep[task] + values * scale[task : task + 1]
        for side in range(2):
            out_codes = []
            for n in range(4):
                values, code = encode(total[n, side * half : (side + 1) * half, :])
                for zh in range(4):
                    out_ref[2 * zh + side, n * half : (n + 1) * half, :] = values[:, zh * wide : (zh + 1) * wide]
                out_codes.append(code)
            out_codes.append(jnp.zeros((EXTRA - 4, width), F32))
            codes = jnp.concatenate(out_codes, axis=0).astype(I32).astype(I16)
            for zh in range(4):
                out_ref[2 * zh + side, 4 * half :, :] = codes[:, zh * wide : (zh + 1) * wide]

    return pl.pallas_call(
        kernel,
        out_shape=jax.ShapeDtypeStruct((8, 4 * half + EXTRA, wide), I16),
        scratch_shapes=[pltpu.VMEM((4, rows, width), F32)],
        compiler_params=params(),
        cost_estimate=pl.CostEstimate(flops=32 * rows * width, bytes_accessed=36 * rows * width, transcendentals=0),
    )(*kept, *arrived)


def lanes(shape, dim):
    return lax.broadcasted_iota(I32, shape, dim)


def gram_kernel(s_ref, in_ref, grads_ref, gram_ref):
    core = s_ref[0]
    rows = (in_ref.shape[1] - EXTRA) // 4
    for zh in range(4):
        near, far = scales(in_ref[2 * zh, 4 * rows :, :]), scales(in_ref[2 * zh + 1, 4 * rows :, :])
        for n in range(4):
            chunk, task = n // 2, n % 2
            at = slice(n * rows, (n + 1) * rows)
            value = floats(in_ref[2 * zh, at, :]) * near[n : n + 1]
            value = value + floats(in_ref[2 * zh + 1, at, :]) * far[n : n + 1]
            mine = 2 * zh + (task + core - 2 * task * core)
            grads_ref[mine, chunk * rows : (chunk + 1) * rows, :] = value

    grads = [grads_ref[t] for t in range(8)]
    lane, sub = lanes((8, 128), 1), lanes((8, 128), 0)
    matrix = jnp.zeros((8, 128), F32)
    for s in range(8):
        for t in range(s, 8):
            product = grads[s] * grads[t]
            folded = product[:, :128] + product[:, 128:]
            total = jnp.sum(jnp.sum(folded, axis=0, keepdims=True), axis=1, keepdims=True)
            here = ((sub == s) & (lane == t)) | ((sub == t) & (lane == s))
            matrix = jnp.where(here, total, matrix)
    line = jnp.zeros((8, 128), F32)
    for s in range(8):
        row = jnp.where(sub == s, matrix, 0.0)
        line = line + (row if s == 0 else pltpu.roll(row, 8 * s, 1))
    flat = jnp.sum(line, axis=0, keepdims=True)
    gram_ref[...] = jnp.broadcast_to(flat, gram_ref.shape)


def gram(table, arrived):
    _, rows, wide = arrived.shape
    rows = (rows - EXTRA) // 2
    return call(
        gram_kernel,
        table,
        (1,),
        (arrived,),
        [whole(arrived.shape)],
        (jax.ShapeDtypeStruct((8, rows, wide), F32), jax.ShapeDtypeStruct((256, 128), F32)),
        (whole((8, rows, wide)), whole((256, 128))),
        [],
        160 * rows * wide,
        32 * rows * wide,
    )


def combine_kernel(s_ref, order_ref, flags_ref, gram_ref, grads_ref, mine_ref, give_ref):
    core = s_ref[0]
    lane, sub = lanes((8, 128), 1), lanes((8, 128), 0)
    flat = jnp.broadcast_to(jnp.sum(gram_ref[...], axis=0, keepdims=True), (8, 128))
    matrix = jnp.zeros((8, 128), F32)
    for s in range(8):
        row = flat if s == 0 else pltpu.roll(flat, 128 - 8 * s, 1)
        matrix = jnp.where((sub == s) & (lane < 8), row, matrix)
    flags = flags_ref[...].astype(F32)
    small = lanes((8, 8), 1)
    coefficients = jnp.where(lane == sub, 1.0, 0.0)
    for k in range(8):
        target = order_ref[k]
        row = jnp.sum(jnp.where(sub == target, matrix, 0.0), axis=0, keepdims=True)
        dots = jnp.sum(coefficients * row, axis=1, keepdims=True)
        square = jnp.sum(jnp.where(lane[:1] == target, row, 0.0), axis=1, keepdims=True)
        active = jnp.sum(jnp.where(small == target, flags, 0.0), axis=1, keepdims=True)
        active = jnp.where(sub[:, :1] == target, 0.0, active)
        removed = jnp.minimum(dots, 0.0) / square * active
        coefficients = coefficients - jnp.where(lane == target, removed, 0.0)
    weights = jnp.sum(coefficients, axis=0, keepdims=True)
    total = None
    for t in range(8):
        weight = jnp.sum(jnp.where(lane[:1] == t, weights, 0.0), axis=1, keepdims=True)
        term = weight * grads_ref[t]
        total = term if total is None else total + term
    left, right = total[:, :128].astype(BF16), total[:, 128:].astype(BF16)

    @pl.when(core == 0)
    def _():
        mine_ref[...] = left
        give_ref[...] = right

    @pl.when(core == 1)
    def _():
        mine_ref[...] = right
        give_ref[...] = left


def combine(table, order, flags, grams, grads):
    rows = grads.shape[1]
    part = jax.ShapeDtypeStruct((rows, 128), BF16)
    return call(
        combine_kernel,
        table,
        (1,),
        (order, flags, grams, grads),
        [pl.BlockSpec(memory_space=pltpu.SMEM), whole((8, 8)), whole((256, 128)), whole(grads.shape)],
        (part, part),
        (whole((rows, 128)),) * 2,
        [],
        20 * rows * 256,
        40 * rows * 256,
    )


def place_kernel(in_ref, out_ref):
    rows = in_ref.shape[1] // 4
    for index, (zl, y, x) in enumerate(itertools.product(range(2), range(4), range(4))):
        co = {"zl": zl, "y": y, "x": x}
        for n in range(4):
            at = (n * 32 + position(co, n // 2, n % 2)) * rows
            out_ref[at : at + rows, :] = in_ref[index, n * rows : (n + 1) * rows, :]


def place(gathered):
    count, rows, cols = gathered.shape
    return pl.pallas_call(
        place_kernel,
        out_shape=jax.ShapeDtypeStruct((count * rows, cols), BF16),
        compiler_params=params(),
        cost_estimate=pl.CostEstimate(flops=0, bytes_accessed=4 * count * rows * cols, transcendentals=0),
    )(gathered)


def on_device(inputs, cotangent, task_order, conflict_flags):
    table = jnp.asarray(device_table())[lax.axis_index(AXES)]
    core = lax.axis_index("core")
    own = cotangent[0]
    other = lax.ppermute(own, "core", [(0, 1), (1, 0)])

    dims = [[(ORDER[0, chunk][n], ORDER[1, chunk][n]) for n in range(5)] for chunk in range(2)]
    slots = [2, 8]
    keys = [(task, chunk) for task in range(2) for chunk in range(2)]
    cots = (own, other)
    arrived, kept = {}, {}
    terms = {}
    for task, chunk in keys:
        start = (2 * core + chunk) * 2 * ROWS
        cot = cots[task] if not terms else after(cots[task], coded)
        terms[task, chunk] = term_of(inputs, start, cot)
        coded = encode_term(table, slots[chunk], terms[task, chunk])
        arrived[task, chunk] = swap_along(coded, dims[chunk][0])
    for at in keys:
        chunk = at[1]
        kept[at], coded = level(table, slots[chunk] + 1, terms[at][None], arrived[at], slots[chunk])
        arrived[at] = swap_along(coded, dims[chunk][1])
    joined, taken = [], []
    for chunk in range(2):
        pair = [(task, chunk) for task in range(2)]
        summed, coded = join_tasks(
            table, slots[chunk] + 2, [kept[at] for at in pair], [arrived[at] for at in pair]
        )
        joined.append(summed)
        taken.append(swap_along(coded, dims[chunk][2]))
    for chunk in range(2):
        joined[chunk], coded = level(table, slots[chunk] + 3, joined[chunk], taken[chunk])
        taken[chunk] = swap_along(coded, dims[chunk][3])
    blocks = line_blocks(joined, taken)
    blocks = lax.all_to_all(blocks, ("zh", "zl"), split_axis=0, concat_axis=0, tiled=True)
    grads, grams = gram(table, blocks)
    grams = lax.all_to_all(grams, AXES, split_axis=0, concat_axis=0, tiled=True)
    mine, give = combine(table, task_order, conflict_flags, grams, grads)
    taken = lax.ppermute(give, "core", [(0, 1), (1, 0)])
    first = jnp.where(core == 0, mine, taken)
    second = jnp.where(core == 0, taken, mine)
    block = jnp.concatenate([first, second], axis=0)
    copies = jnp.broadcast_to(block, (32, *block.shape))
    gathered = lax.all_to_all(copies, DP, split_axis=0, concat_axis=0, tiled=True)
    return place(gathered)


def solution(mesh):
    split = Mesh(mesh.devices.reshape(SIZES), AXES)
    placed = (P(DP, None), P(TASK, DP, None), P(), P())
    return jax.shard_map(
        on_device, mesh=split, in_specs=placed, out_specs=P(None, TASK), check_vma=False
    )
```

```python
import itertools

import jax
import jax.numpy as jnp
import numpy as np
from jax import lax
from jax.experimental import pallas as pl
from jax.experimental.pallas import tpu as pltpu
from jax.sharding import Mesh
from jax.sharding import PartitionSpec as P

AXES = ("zh", "core", "zl", "y", "x")
SIZES = (4, 2, 2, 4, 4)
DP = ("zl", "y", "x")
TASK = ("zh", "core")
F32, BF16, I16, I32 = jnp.float32, jnp.bfloat16, jnp.int16, jnp.int32

PARTNER = {"a": (1, 0, 3, 2), "b": (3, 2, 1, 0)}
BIT = {"a": (0, 1, 1, 0), "b": (0, 0, 1, 1)}
ORDER = {
    (0, 0): ("xa", "yb", "xb", "ya", "z"),
    (0, 1): ("yb", "xa", "ya", "xb", "z"),
    (1, 0): ("ya", "xb", "xa", "yb", "z"),
    (1, 1): ("xb", "ya", "yb", "xa", "z"),
}
FULL = 32000.0
STEPS = 64.0
EXTRA = 16


def coordinates():
    return [dict(zip(AXES, v)) for v in itertools.product(*map(range, SIZES))]


def linear(co):
    index = 0
    for axis, size in zip(AXES, SIZES):
        index = index * size + co[axis]
    return index


def bit_of(co, dim):
    return co["zl"] if dim == "z" else BIT[dim[1]][co[dim[0]]]


def partner(co, dim):
    if dim == "z":
        return {**co, "zl": 1 - co["zl"]}
    return {**co, dim[0]: PARTNER[dim[1]][co[dim[0]]]}


def swap_along(value, dims):
    pairs = [(linear(co), linear(partner(co, dims[co["core"]]))) for co in coordinates()]
    return lax.ppermute(value, AXES, pairs)


def position(co, core, chunk):
    place = 0
    for dim in ORDER[core, chunk]:
        place = 2 * place + bit_of(co, dim)
    return place


def device_table():
    rows = []
    for co in coordinates():
        core = co["core"]
        row = [core, co["zh"]]
        for chunk in range(2):
            bits = [bit_of(co, dim) for dim in ORDER[core, chunk]]
            row += bits + [0]
        rows.append(row + [0] * (16 - len(row)))
    return np.asarray(rows, np.int32)


def encode(tile):
    top = jnp.maximum(jnp.max(jnp.abs(tile), axis=0, keepdims=True), 1e-30)
    code = jnp.ceil(jnp.log(top) * STEPS)
    values = jnp.round(tile * (jnp.exp(code * (-1.0 / STEPS)) * FULL))
    return values.astype(I32).astype(I16), code


def scales(codes):
    return jnp.exp(codes.astype(I32).astype(F32) * (1.0 / STEPS)) * (1.0 / FULL)


def floats(values):
    return values.astype(I32).astype(F32)


def params(mib=14):
    return pltpu.CompilerParams(vmem_limit_bytes=mib << 20)


def call(kernel, scalars, grid, inputs, in_specs, out_shape, out_specs, scratch, flops, nbytes, **extra):
    return pl.pallas_call(
        kernel,
        out_shape=out_shape,
        grid_spec=pltpu.PrefetchScalarGridSpec(
            num_scalar_prefetch=1,
            grid=grid,
            in_specs=in_specs,
            out_specs=out_specs,
            scratch_shapes=scratch,
        ),
        compiler_params=params(),
        cost_estimate=pl.CostEstimate(flops=flops, bytes_accessed=nbytes, transcendentals=0),
        **extra,
    )(scalars, *inputs)


def whole(shape):
    return pl.BlockSpec(shape, lambda *_: (0,) * len(shape))


ROWS = 512
TILE = 128


def encode_kernel(s_ref, term_ref, out_ref, codes):
    tile = pl.program_id(0)
    values, code = encode(term_ref[...])
    out_ref[pl.ds(pl.multiple_of(tile * TILE, TILE), TILE), :] = values
    codes[pl.ds(tile, 1), :] = code

    @pl.when(tile == ROWS // TILE - 1)
    def _():
        out_ref[ROWS:, :] = codes[...].astype(I32).astype(I16)


def encode_term(table, slot, term):
    rows, width = ROWS, term.shape[1]
    per = rows // TILE
    return call(
        encode_kernel,
        table,
        (per,),
        (term,),
        [pl.BlockSpec((TILE, width), lambda n, s: ((1 - s[slot]) * per + n, 0))],
        jax.ShapeDtypeStruct((rows + EXTRA, width), I16),
        whole((rows + EXTRA, width)),
        [pltpu.VMEM((EXTRA, width), F32)],
        8 * rows * width,
        6 * rows * width,
    )


def term_of(inputs, start, cot):
    part = lax.dynamic_slice(inputs, (0, start), (inputs.shape[0], 2 * ROWS))
    return lax.dot_general(part, cot, (((0,), (0,)), ((), ())), preferred_element_type=F32)


def after(value, *others):
    return lax.optimization_barrier((value, *others))[0]


def level(table, slot, kept, arrived, first=None):
    tasks, rows, width = kept.shape
    rows = rows if first is None else rows // 2
    half = rows // 2
    tile = min(TILE, half)
    per = half // tile
    code_rows = min(TILE, rows)

    def skip(s):
        return 0 if first is None else s[first] * 2 * per

    def kernel(s_ref, keep_ref, give_ref, keep_in, give_in, codes_ref, sum_ref, out_ref, scale, codes):
        task, j = pl.program_id(0), pl.program_id(1)
        bit = s_ref[slot]

        @pl.when((task == 0) & (j == 0))
        def _():
            scale[...] = scales(codes_ref[...])
            codes[...] = jnp.zeros_like(codes)

        def row_of(side):
            return (task * rows + side * half + j * tile) // code_rows

        give = give_ref[0] + floats(give_in[...]) * scale[pl.ds(row_of(1 - bit), 1), :]
        values, code = encode(give)
        at = task * per + j
        out_ref[pl.ds(pl.multiple_of(at * tile, tile), tile), :] = values
        codes[pl.ds(at, 1), :] = code
        sum_ref[0] = keep_ref[0] + floats(keep_in[...]) * scale[pl.ds(row_of(bit), 1), :]

        @pl.when((task == tasks - 1) & (j == per - 1))
        def _():
            out_ref[tasks * half :, :] = codes[...].astype(I32).astype(I16)

    return call(
        kernel,
        table,
        (tasks, per),
        (kept, kept, arrived, arrived, arrived),
        [
            pl.BlockSpec((1, tile, width), lambda t, j, s: (t, skip(s) + s[slot] * per + j, 0)),
            pl.BlockSpec((1, tile, width), lambda t, j, s: (t, skip(s) + (1 - s[slot]) * per + j, 0)),
            pl.BlockSpec((tile, width), lambda t, j, s: ((2 * t + s[slot]) * per + j, 0)),
            pl.BlockSpec((tile, width), lambda t, j, s: ((2 * t + 1 - s[slot]) * per + j, 0)),
            pl.BlockSpec((EXTRA, width), lambda t, j, s: (tasks * rows // EXTRA, 0)),
        ],
        (
            jax.ShapeDtypeStruct((tasks, half, width), F32),
            jax.ShapeDtypeStruct((tasks * half + EXTRA, width), I16),
        ),
        (pl.BlockSpec((1, tile, width), lambda t, j, s: (t, j, 0)), whole((tasks * half + EXTRA, width))),
        [pltpu.VMEM((EXTRA, width), F32), pltpu.VMEM((EXTRA, width), F32)],
        8 * tasks * rows * width,
        tasks * rows * width * 9,
    )


def join_tasks(table, slot, kept, arrived):
    _, rows, width = kept[0].shape
    half = rows // 2

    def kernel(s_ref, keep_a, keep_b, in_a, in_b, sum_ref, out_ref, scale):
        bit = s_ref[slot]
        out_codes = []
        for task, (keep, arr) in enumerate(((keep_a, in_a), (keep_b, in_b))):
            scale[...] = scales(arr[rows:, :])

            def part(side):
                at = pl.ds(pl.multiple_of(side * half, half), half)
                return keep[0, at, :] + floats(arr[at, :]) * scale[pl.ds(side * half // TILE, 1), :]

            values, code = encode(part(1 - bit))
            out_ref[task * half : (task + 1) * half, :] = values
            out_codes.append(code)
            sum_ref[task] = part(bit)
        out_codes.append(jnp.zeros((EXTRA - 2, width), F32))
        out_ref[2 * half :, :] = jnp.concatenate(out_codes, axis=0).astype(I32).astype(I16)

    shapes = ((1, rows, width), (1, rows, width), (rows + EXTRA, width), (rows + EXTRA, width))
    return call(
        kernel,
        table,
        (1,),
        (*kept, *arrived),
        [whole(s) for s in shapes],
        (jax.ShapeDtypeStruct((2, half, width), F32), jax.ShapeDtypeStruct((2 * half + EXTRA, width), I16)),
        (whole((2, half, width)), whole((2 * half + EXTRA, width))),
        [pltpu.VMEM((EXTRA, width), F32)],
        16 * rows * width,
        2 * rows * width * 9,
    )


def line_blocks(kept, arrived):
    _, rows, width = kept[0].shape
    half, wide = rows // 2, width // 4

    def kernel(keep_a, keep_b, in_a, in_b, out_ref, total):
        for chunk, (keep, arr) in enumerate(((keep_a, in_a), (keep_b, in_b))):
            scale = scales(arr[2 * rows :, :])
            for task in range(2):
                values = floats(arr[task * rows : (task + 1) * rows, :])
                total[2 * chunk + task] = keep[task] + values * scale[task : task + 1]
        for side in range(2):
            out_codes = []
            for n in range(4):
                values, code = encode(total[n, side * half : (side + 1) * half, :])
                for zh in range(4):
                    out_ref[2 * zh + side, n * half : (n + 1) * half, :] = values[:, zh * wide : (zh + 1) * wide]
                out_codes.append(code)
            out_codes.append(jnp.zeros((EXTRA - 4, width), F32))
            codes = jnp.concatenate(out_codes, axis=0).astype(I32).astype(I16)
            for zh in range(4):
                out_ref[2 * zh + side, 4 * half :, :] = codes[:, zh * wide : (zh + 1) * wide]

    return pl.pallas_call(
        kernel,
        out_shape=jax.ShapeDtypeStruct((8, 4 * half + EXTRA, wide), I16),
        scratch_shapes=[pltpu.VMEM((4, rows, width), F32)],
        compiler_params=params(),
        cost_estimate=pl.CostEstimate(flops=32 * rows * width, bytes_accessed=36 * rows * width, transcendentals=0),
    )(*kept, *arrived)


def lanes(shape, dim):
    return lax.broadcasted_iota(I32, shape, dim)


def gram_kernel(s_ref, in_ref, grads_ref, gram_ref):
    core = s_ref[0]
    rows = (in_ref.shape[1] - EXTRA) // 4
    for zh in range(4):
        near, far = scales(in_ref[2 * zh, 4 * rows :, :]), scales(in_ref[2 * zh + 1, 4 * rows :, :])
        for n in range(4):
            chunk, task = n // 2, n % 2
            at = slice(n * rows, (n + 1) * rows)
            value = floats(in_ref[2 * zh, at, :]) * near[n : n + 1]
            value = value + floats(in_ref[2 * zh + 1, at, :]) * far[n : n + 1]
            mine = 2 * zh + (task + core - 2 * task * core)
            grads_ref[mine, chunk * rows : (chunk + 1) * rows, :] = value

    grads = [grads_ref[t] for t in range(8)]
    lane, sub = lanes((8, 128), 1), lanes((8, 128), 0)
    matrix = jnp.zeros((8, 128), F32)
    for s in range(8):
        for t in range(s, 8):
            product = grads[s] * grads[t]
            folded = product[:, :128] + product[:, 128:]
            total = jnp.sum(jnp.sum(folded, axis=0, keepdims=True), axis=1, keepdims=True)
            here = ((sub == s) & (lane == t)) | ((sub == t) & (lane == s))
            matrix = jnp.where(here, total, matrix)
    line = jnp.zeros((8, 128), F32)
    for s in range(8):
        row = jnp.where(sub == s, matrix, 0.0)
        line = line + (row if s == 0 else pltpu.roll(row, 8 * s, 1))
    flat = jnp.sum(line, axis=0, keepdims=True)
    gram_ref[...] = jnp.broadcast_to(flat, gram_ref.shape)


def gram(table, arrived):
    _, rows, wide = arrived.shape
    rows = (rows - EXTRA) // 2
    return call(
        gram_kernel,
        table,
        (1,),
        (arrived,),
        [whole(arrived.shape)],
        (jax.ShapeDtypeStruct((8, rows, wide), F32), jax.ShapeDtypeStruct((256, 128), F32)),
        (whole((8, rows, wide)), whole((256, 128))),
        [],
        160 * rows * wide,
        32 * rows * wide,
    )


def combine_kernel(s_ref, order_ref, flags_ref, gram_ref, grads_ref, mine_ref, give_ref):
    core = s_ref[0]
    lane, sub = lanes((8, 128), 1), lanes((8, 128), 0)
    flat = jnp.broadcast_to(jnp.sum(gram_ref[...], axis=0, keepdims=True), (8, 128))
    matrix = jnp.zeros((8, 128), F32)
    for s in range(8):
        row = flat if s == 0 else pltpu.roll(flat, 128 - 8 * s, 1)
        matrix = jnp.where((sub == s) & (lane < 8), row, matrix)
    flags = flags_ref[...].astype(F32)
    small = lanes((8, 8), 1)
    coefficients = jnp.where(lane == sub, 1.0, 0.0)
    for k in range(8):
        target = order_ref[k]
        row = jnp.sum(jnp.where(sub == target, matrix, 0.0), axis=0, keepdims=True)
        dots = jnp.sum(coefficients * row, axis=1, keepdims=True)
        square = jnp.sum(jnp.where(lane[:1] == target, row, 0.0), axis=1, keepdims=True)
        active = jnp.sum(jnp.where(small == target, flags, 0.0), axis=1, keepdims=True)
        active = jnp.where(sub[:, :1] == target, 0.0, active)
        removed = jnp.minimum(dots, 0.0) / square * active
        coefficients = coefficients - jnp.where(lane == target, removed, 0.0)
    weights = jnp.sum(coefficients, axis=0, keepdims=True)
    total = None
    for t in range(8):
        weight = jnp.sum(jnp.where(lane[:1] == t, weights, 0.0), axis=1, keepdims=True)
        term = weight * grads_ref[t]
        total = term if total is None else total + term
    left, right = total[:, :128].astype(BF16), total[:, 128:].astype(BF16)

    @pl.when(core == 0)
    def _():
        mine_ref[...] = left
        give_ref[...] = right

    @pl.when(core == 1)
    def _():
        mine_ref[...] = right
        give_ref[...] = left


def combine(table, order, flags, grams, grads):
    rows = grads.shape[1]
    part = jax.ShapeDtypeStruct((rows, 128), BF16)
    return call(
        combine_kernel,
        table,
        (1,),
        (order, flags, grams, grads),
        [pl.BlockSpec(memory_space=pltpu.SMEM), whole((8, 8)), whole((256, 128)), whole(grads.shape)],
        (part, part),
        (whole((rows, 128)),) * 2,
        [],
        20 * rows * 256,
        40 * rows * 256,
    )


def place_kernel(in_ref, out_ref):
    rows = in_ref.shape[1] // 4
    for index, (zl, y, x) in enumerate(itertools.product(range(2), range(4), range(4))):
        co = {"zl": zl, "y": y, "x": x}
        for n in range(4):
            at = (n * 32 + position(co, n // 2, n % 2)) * rows
            out_ref[at : at + rows, :] = in_ref[index, n * rows : (n + 1) * rows, :]


def place(gathered):
    count, rows, cols = gathered.shape
    return pl.pallas_call(
        place_kernel,
        out_shape=jax.ShapeDtypeStruct((count * rows, cols), BF16),
        compiler_params=params(),
        cost_estimate=pl.CostEstimate(flops=0, bytes_accessed=4 * count * rows * cols, transcendentals=0),
    )(gathered)


def on_device(inputs, cotangent, task_order, conflict_flags):
    table = jnp.asarray(device_table())[lax.axis_index(AXES)]
    core = lax.axis_index("core")
    own = cotangent[0]
    other = lax.ppermute(own, "core", [(0, 1), (1, 0)])

    dims = [[(ORDER[0, chunk][n], ORDER[1, chunk][n]) for n in range(5)] for chunk in range(2)]
    slots = [2, 8]
    keys = [(task, chunk) for task in range(2) for chunk in range(2)]
    cots = (own, other)
    arrived, kept = {}, {}
    terms = {}
    for task, chunk in keys:
        start = (2 * core + chunk) * 2 * ROWS
        cot = cots[task] if not terms else after(cots[task], coded)
        terms[task, chunk] = term_of(inputs, start, cot)
        coded = encode_term(table, slots[chunk], terms[task, chunk])
        arrived[task, chunk] = swap_along(coded, dims[chunk][0])
    for at in keys:
        chunk = at[1]
        kept[at], coded = level(table, slots[chunk] + 1, terms[at][None], arrived[at], slots[chunk])
        arrived[at] = swap_along(coded, dims[chunk][1])
    joined, taken = {}, {}
    for chunk in (1, 0):
        pair = [(task, chunk) for task in range(2)]
        sums = [kept[at] for at in pair]
        if chunk == 0:
            sums[0] = after(sums[0], coded)
        joined[chunk], coded = join_tasks(table, slots[chunk] + 2, sums, [arrived[at] for at in pair])
        taken[chunk] = swap_along(coded, dims[chunk][2])
    for chunk in (1, 0):
        if chunk == 0:
            joined[chunk] = after(joined[chunk], coded)
        joined[chunk], coded = level(table, slots[chunk] + 3, joined[chunk], taken[chunk])
        taken[chunk] = swap_along(coded, dims[chunk][3])
    blocks = line_blocks([joined[0], joined[1]], [taken[0], taken[1]])
    blocks = lax.all_to_all(blocks, ("zh", "zl"), split_axis=0, concat_axis=0, tiled=True)
    grads, grams = gram(table, blocks)
    grams = lax.all_to_all(grams, AXES, split_axis=0, concat_axis=0, tiled=True)
    mine, give = combine(table, task_order, conflict_flags, grams, grads)
    taken = lax.ppermute(give, "core", [(0, 1), (1, 0)])
    first = jnp.where(core == 0, mine, taken)
    second = jnp.where(core == 0, taken, mine)
    block = jnp.concatenate([first, second], axis=0)
    copies = jnp.broadcast_to(block, (32, *block.shape))
    gathered = lax.all_to_all(copies, DP, split_axis=0, concat_axis=0, tiled=True)
    return place(gathered)


def solution(mesh):
    split = Mesh(mesh.devices.reshape(SIZES), AXES)
    placed = (P(DP, None), P(TASK, DP, None), P(), P())
    return jax.shard_map(
        on_device, mesh=split, in_specs=placed, out_specs=P(None, TASK), check_vma=False
    )
```

```python
import itertools

import jax
import jax.numpy as jnp
import numpy as np
from jax import lax
from jax.experimental import pallas as pl
from jax.experimental.pallas import tpu as pltpu
from jax.sharding import Mesh
from jax.sharding import PartitionSpec as P

AXES = ("zh", "core", "zl", "y", "x")
SIZES = (4, 2, 2, 4, 4)
DP = ("zl", "y", "x")
TASK = ("zh", "core")
F32, BF16, I16, I32 = jnp.float32, jnp.bfloat16, jnp.int16, jnp.int32

PARTNER = {"a": (1, 0, 3, 2), "b": (3, 2, 1, 0)}
BIT = {"a": (0, 1, 1, 0), "b": (0, 0, 1, 1)}
ORDER = {
    (0, 0): ("xa", "ya", "xb", "yb", "z"),
    (0, 1): ("yb", "xb", "ya", "xa", "z"),
    (1, 0): ("ya", "xa", "yb", "xb", "z"),
    (1, 1): ("xb", "yb", "xa", "ya", "z"),
}
FULL = 32000.0
STEPS = 64.0
EXTRA = 16


def coordinates():
    return [dict(zip(AXES, v)) for v in itertools.product(*map(range, SIZES))]


def linear(co):
    index = 0
    for axis, size in zip(AXES, SIZES):
        index = index * size + co[axis]
    return index


def bit_of(co, dim):
    return co["zl"] if dim == "z" else BIT[dim[1]][co[dim[0]]]


def partner(co, dim):
    if dim == "z":
        return {**co, "zl": 1 - co["zl"]}
    return {**co, dim[0]: PARTNER[dim[1]][co[dim[0]]]}


def swap_along(value, dims):
    pairs = [(linear(co), linear(partner(co, dims[co["core"]]))) for co in coordinates()]
    return lax.ppermute(value, AXES, pairs)


def position(co, core, chunk):
    place = 0
    for dim in ORDER[core, chunk]:
        place = 2 * place + bit_of(co, dim)
    return place


def device_table():
    rows = []
    for co in coordinates():
        core = co["core"]
        row = [core, co["zh"]]
        for chunk in range(2):
            bits = [bit_of(co, dim) for dim in ORDER[core, chunk]]
            row += bits + [0]
        rows.append(row + [0] * (16 - len(row)))
    return np.asarray(rows, np.int32)


def encode(tile):
    top = jnp.maximum(jnp.max(jnp.abs(tile), axis=0, keepdims=True), 1e-30)
    code = jnp.ceil(jnp.log(top) * STEPS)
    values = jnp.round(tile * (jnp.exp(code * (-1.0 / STEPS)) * FULL))
    return values.astype(I32).astype(I16), code


def scales(codes):
    return jnp.exp(codes.astype(I32).astype(F32) * (1.0 / STEPS)) * (1.0 / FULL)


def floats(values):
    return values.astype(I32).astype(F32)


def params(mib=14):
    return pltpu.CompilerParams(vmem_limit_bytes=mib << 20)


def call(kernel, scalars, grid, inputs, in_specs, out_shape, out_specs, scratch, flops, nbytes, **extra):
    return pl.pallas_call(
        kernel,
        out_shape=out_shape,
        grid_spec=pltpu.PrefetchScalarGridSpec(
            num_scalar_prefetch=1,
            grid=grid,
            in_specs=in_specs,
            out_specs=out_specs,
            scratch_shapes=scratch,
        ),
        compiler_params=params(),
        cost_estimate=pl.CostEstimate(flops=flops, bytes_accessed=nbytes, transcendentals=0),
        **extra,
    )(scalars, *inputs)


def whole(shape):
    return pl.BlockSpec(shape, lambda *_: (0,) * len(shape))


ROWS = 512
TILE = 128


def encode_kernel(s_ref, term_ref, out_ref, codes):
    tile = pl.program_id(0)
    values, code = encode(term_ref[...])
    out_ref[pl.ds(pl.multiple_of(tile * TILE, TILE), TILE), :] = values
    codes[pl.ds(tile, 1), :] = code

    @pl.when(tile == ROWS // TILE - 1)
    def _():
        out_ref[ROWS:, :] = codes[...].astype(I32).astype(I16)


def encode_term(table, slot, term):
    rows, width = ROWS, term.shape[1]
    per = rows // TILE
    return call(
        encode_kernel,
        table,
        (per,),
        (term,),
        [pl.BlockSpec((TILE, width), lambda n, s: ((1 - s[slot]) * per + n, 0))],
        jax.ShapeDtypeStruct((rows + EXTRA, width), I16),
        whole((rows + EXTRA, width)),
        [pltpu.VMEM((EXTRA, width), F32)],
        8 * rows * width,
        6 * rows * width,
    )


def term_of(inputs, start, cot):
    part = lax.dynamic_slice(inputs, (0, start), (inputs.shape[0], 2 * ROWS))
    return lax.dot_general(part, cot, (((0,), (0,)), ((), ())), preferred_element_type=F32)


def after(value, *others):
    return lax.optimization_barrier((value, *others))[0]


def level(table, slot, kept, arrived, first=None):
    tasks, rows, width = kept.shape
    rows = rows if first is None else rows // 2
    half = rows // 2
    tile = min(TILE, half)
    per = half // tile
    code_rows = min(TILE, rows)

    def skip(s):
        return 0 if first is None else s[first] * 2 * per

    def kernel(s_ref, keep_ref, give_ref, keep_in, give_in, codes_ref, sum_ref, out_ref, scale, codes):
        task, j = pl.program_id(0), pl.program_id(1)
        bit = s_ref[slot]

        @pl.when((task == 0) & (j == 0))
        def _():
            scale[...] = scales(codes_ref[...])
            codes[...] = jnp.zeros_like(codes)

        def row_of(side):
            return (task * rows + side * half + j * tile) // code_rows

        give = give_ref[0] + floats(give_in[...]) * scale[pl.ds(row_of(1 - bit), 1), :]
        values, code = encode(give)
        at = task * per + j
        out_ref[pl.ds(pl.multiple_of(at * tile, tile), tile), :] = values
        codes[pl.ds(at, 1), :] = code
        sum_ref[0] = keep_ref[0] + floats(keep_in[...]) * scale[pl.ds(row_of(bit), 1), :]

        @pl.when((task == tasks - 1) & (j == per - 1))
        def _():
            out_ref[tasks * half :, :] = codes[...].astype(I32).astype(I16)

    return call(
        kernel,
        table,
        (tasks, per),
        (kept, kept, arrived, arrived, arrived),
        [
            pl.BlockSpec((1, tile, width), lambda t, j, s: (t, skip(s) + s[slot] * per + j, 0)),
            pl.BlockSpec((1, tile, width), lambda t, j, s: (t, skip(s) + (1 - s[slot]) * per + j, 0)),
            pl.BlockSpec((tile, width), lambda t, j, s: ((2 * t + s[slot]) * per + j, 0)),
            pl.BlockSpec((tile, width), lambda t, j, s: ((2 * t + 1 - s[slot]) * per + j, 0)),
            pl.BlockSpec((EXTRA, width), lambda t, j, s: (tasks * rows // EXTRA, 0)),
        ],
        (
            jax.ShapeDtypeStruct((tasks, half, width), F32),
            jax.ShapeDtypeStruct((tasks * half + EXTRA, width), I16),
        ),
        (pl.BlockSpec((1, tile, width), lambda t, j, s: (t, j, 0)), whole((tasks * half + EXTRA, width))),
        [pltpu.VMEM((EXTRA, width), F32), pltpu.VMEM((EXTRA, width), F32)],
        8 * tasks * rows * width,
        tasks * rows * width * 9,
    )


def join_tasks(table, slot, kept, arrived):
    _, rows, width = kept[0].shape
    half = rows // 2

    def kernel(s_ref, keep_a, keep_b, in_a, in_b, sum_ref, out_ref, scale):
        bit = s_ref[slot]
        out_codes = []
        for task, (keep, arr) in enumerate(((keep_a, in_a), (keep_b, in_b))):
            scale[...] = scales(arr[rows:, :])

            def part(side):
                at = pl.ds(pl.multiple_of(side * half, half), half)
                return keep[0, at, :] + floats(arr[at, :]) * scale[pl.ds(side * half // TILE, 1), :]

            values, code = encode(part(1 - bit))
            out_ref[task * half : (task + 1) * half, :] = values
            out_codes.append(code)
            sum_ref[task] = part(bit)
        out_codes.append(jnp.zeros((EXTRA - 2, width), F32))
        out_ref[2 * half :, :] = jnp.concatenate(out_codes, axis=0).astype(I32).astype(I16)

    shapes = ((1, rows, width), (1, rows, width), (rows + EXTRA, width), (rows + EXTRA, width))
    return call(
        kernel,
        table,
        (1,),
        (*kept, *arrived),
        [whole(s) for s in shapes],
        (jax.ShapeDtypeStruct((2, half, width), F32), jax.ShapeDtypeStruct((2 * half + EXTRA, width), I16)),
        (whole((2, half, width)), whole((2 * half + EXTRA, width))),
        [pltpu.VMEM((EXTRA, width), F32)],
        16 * rows * width,
        2 * rows * width * 9,
    )


def line_blocks(kept, arrived):
    _, rows, width = kept[0].shape
    half, wide = rows // 2, width // 4

    def kernel(keep_a, keep_b, in_a, in_b, out_ref, total):
        for chunk, (keep, arr) in enumerate(((keep_a, in_a), (keep_b, in_b))):
            scale = scales(arr[2 * rows :, :])
            for task in range(2):
                values = floats(arr[task * rows : (task + 1) * rows, :])
                total[2 * chunk + task] = keep[task] + values * scale[task : task + 1]
        for side in range(2):
            out_codes = []
            for n in range(4):
                values, code = encode(total[n, side * half : (side + 1) * half, :])
                for zh in range(4):
                    out_ref[2 * zh + side, n * half : (n + 1) * half, :] = values[:, zh * wide : (zh + 1) * wide]
                out_codes.append(code)
            out_codes.append(jnp.zeros((EXTRA - 4, width), F32))
            codes = jnp.concatenate(out_codes, axis=0).astype(I32).astype(I16)
            for zh in range(4):
                out_ref[2 * zh + side, 4 * half :, :] = codes[:, zh * wide : (zh + 1) * wide]

    return pl.pallas_call(
        kernel,
        out_shape=jax.ShapeDtypeStruct((8, 4 * half + EXTRA, wide), I16),
        scratch_shapes=[pltpu.VMEM((4, rows, width), F32)],
        compiler_params=params(),
        cost_estimate=pl.CostEstimate(flops=32 * rows * width, bytes_accessed=36 * rows * width, transcendentals=0),
    )(*kept, *arrived)


def lanes(shape, dim):
    return lax.broadcasted_iota(I32, shape, dim)


def gram_kernel(s_ref, in_ref, grads_ref, gram_ref):
    core = s_ref[0]
    rows = (in_ref.shape[1] - EXTRA) // 4
    for zh in range(4):
        near, far = scales(in_ref[2 * zh, 4 * rows :, :]), scales(in_ref[2 * zh + 1, 4 * rows :, :])
        for n in range(4):
            chunk, task = n // 2, n % 2
            at = slice(n * rows, (n + 1) * rows)
            value = floats(in_ref[2 * zh, at, :]) * near[n : n + 1]
            value = value + floats(in_ref[2 * zh + 1, at, :]) * far[n : n + 1]
            mine = 2 * zh + (task + core - 2 * task * core)
            grads_ref[mine, chunk * rows : (chunk + 1) * rows, :] = value

    grads = [grads_ref[t] for t in range(8)]
    lane, sub = lanes((8, 128), 1), lanes((8, 128), 0)
    matrix = jnp.zeros((8, 128), F32)
    for s in range(8):
        for t in range(s, 8):
            product = grads[s] * grads[t]
            folded = product[:, :128] + product[:, 128:]
            total = jnp.sum(jnp.sum(folded, axis=0, keepdims=True), axis=1, keepdims=True)
            here = ((sub == s) & (lane == t)) | ((sub == t) & (lane == s))
            matrix = jnp.where(here, total, matrix)
    line = jnp.zeros((8, 128), F32)
    for s in range(8):
        row = jnp.where(sub == s, matrix, 0.0)
        line = line + (row if s == 0 else pltpu.roll(row, 8 * s, 1))
    flat = jnp.sum(line, axis=0, keepdims=True)
    gram_ref[...] = jnp.broadcast_to(flat, gram_ref.shape)


def gram(table, arrived):
    _, rows, wide = arrived.shape
    rows = (rows - EXTRA) // 2
    return call(
        gram_kernel,
        table,
        (1,),
        (arrived,),
        [whole(arrived.shape)],
        (jax.ShapeDtypeStruct((8, rows, wide), F32), jax.ShapeDtypeStruct((256, 128), F32)),
        (whole((8, rows, wide)), whole((256, 128))),
        [],
        160 * rows * wide,
        32 * rows * wide,
    )


def combine_kernel(s_ref, order_ref, flags_ref, gram_ref, grads_ref, mine_ref, give_ref):
    core = s_ref[0]
    lane, sub = lanes((8, 128), 1), lanes((8, 128), 0)
    flat = jnp.broadcast_to(jnp.sum(gram_ref[...], axis=0, keepdims=True), (8, 128))
    matrix = jnp.zeros((8, 128), F32)
    for s in range(8):
        row = flat if s == 0 else pltpu.roll(flat, 128 - 8 * s, 1)
        matrix = jnp.where((sub == s) & (lane < 8), row, matrix)
    flags = flags_ref[...].astype(F32)
    small = lanes((8, 8), 1)
    coefficients = jnp.where(lane == sub, 1.0, 0.0)
    for k in range(8):
        target = order_ref[k]
        row = jnp.sum(jnp.where(sub == target, matrix, 0.0), axis=0, keepdims=True)
        dots = jnp.sum(coefficients * row, axis=1, keepdims=True)
        square = jnp.sum(jnp.where(lane[:1] == target, row, 0.0), axis=1, keepdims=True)
        active = jnp.sum(jnp.where(small == target, flags, 0.0), axis=1, keepdims=True)
        active = jnp.where(sub[:, :1] == target, 0.0, active)
        removed = jnp.minimum(dots, 0.0) / square * active
        coefficients = coefficients - jnp.where(lane == target, removed, 0.0)
    weights = jnp.sum(coefficients, axis=0, keepdims=True)
    total = None
    for t in range(8):
        weight = jnp.sum(jnp.where(lane[:1] == t, weights, 0.0), axis=1, keepdims=True)
        term = weight * grads_ref[t]
        total = term if total is None else total + term
    left, right = total[:, :128].astype(BF16), total[:, 128:].astype(BF16)

    @pl.when(core == 0)
    def _():
        mine_ref[...] = left
        give_ref[...] = right

    @pl.when(core == 1)
    def _():
        mine_ref[...] = right
        give_ref[...] = left


def combine(table, order, flags, grams, grads):
    rows = grads.shape[1]
    part = jax.ShapeDtypeStruct((rows, 128), BF16)
    return call(
        combine_kernel,
        table,
        (1,),
        (order, flags, grams, grads),
        [pl.BlockSpec(memory_space=pltpu.SMEM), whole((8, 8)), whole((256, 128)), whole(grads.shape)],
        (part, part),
        (whole((rows, 128)),) * 2,
        [],
        20 * rows * 256,
        40 * rows * 256,
    )


def place_kernel(in_ref, out_ref):
    rows = in_ref.shape[1] // 4
    for index, (zl, y, x) in enumerate(itertools.product(range(2), range(4), range(4))):
        co = {"zl": zl, "y": y, "x": x}
        for n in range(4):
            at = (n * 32 + position(co, n // 2, n % 2)) * rows
            out_ref[at : at + rows, :] = in_ref[index, n * rows : (n + 1) * rows, :]


def place(gathered):
    count, rows, cols = gathered.shape
    return pl.pallas_call(
        place_kernel,
        out_shape=jax.ShapeDtypeStruct((count * rows, cols), BF16),
        compiler_params=params(),
        cost_estimate=pl.CostEstimate(flops=0, bytes_accessed=4 * count * rows * cols, transcendentals=0),
    )(gathered)


def on_device(inputs, cotangent, task_order, conflict_flags):
    table = jnp.asarray(device_table())[lax.axis_index(AXES)]
    core = lax.axis_index("core")
    own = cotangent[0]
    other = lax.ppermute(own, "core", [(0, 1), (1, 0)])

    dims = [[(ORDER[0, chunk][n], ORDER[1, chunk][n]) for n in range(5)] for chunk in range(2)]
    slots = [2, 8]
    keys = [(task, chunk) for task in range(2) for chunk in range(2)]
    cots = (own, other)
    arrived, kept = {}, {}
    terms = {}
    for task, chunk in keys:
        start = (2 * core + chunk) * 2 * ROWS
        cot = cots[task] if not terms else after(cots[task], coded)
        terms[task, chunk] = term_of(inputs, start, cot)
        coded = encode_term(table, slots[chunk], terms[task, chunk])
        arrived[task, chunk] = swap_along(coded, dims[chunk][0])
    for at in keys:
        chunk = at[1]
        kept[at], coded = level(table, slots[chunk] + 1, terms[at][None], arrived[at], slots[chunk])
        arrived[at] = swap_along(coded, dims[chunk][1])
    joined, taken = [], []
    for chunk in range(2):
        pair = [(task, chunk) for task in range(2)]
        sums = [kept[at] for at in pair]
        if chunk:
            sums[0] = after(sums[0], coded)
        summed, coded = join_tasks(table, slots[chunk] + 2, sums, [arrived[at] for at in pair])
        joined.append(summed)
        taken.append(swap_along(coded, dims[chunk][2]))
    for chunk in range(2):
        if chunk:
            joined[chunk] = after(joined[chunk], coded)
        joined[chunk], coded = level(table, slots[chunk] + 3, joined[chunk], taken[chunk])
        taken[chunk] = swap_along(coded, dims[chunk][3])
    blocks = line_blocks(joined, taken)
    blocks = lax.all_to_all(blocks, ("zh", "zl"), split_axis=0, concat_axis=0, tiled=True)
    grads, grams = gram(table, blocks)
    grams = lax.all_to_all(grams, AXES, split_axis=0, concat_axis=0, tiled=True)
    mine, give = combine(table, task_order, conflict_flags, grams, grads)
    taken = lax.ppermute(give, "core", [(0, 1), (1, 0)])
    first = jnp.where(core == 0, mine, taken)
    second = jnp.where(core == 0, taken, mine)
    block = jnp.concatenate([first, second], axis=0)
    copies = jnp.broadcast_to(block, (32, *block.shape))
    gathered = lax.all_to_all(copies, DP, split_axis=0, concat_axis=0, tiled=True)
    return place(gathered)


def solution(mesh):
    split = Mesh(mesh.devices.reshape(SIZES), AXES)
    placed = (P(DP, None), P(TASK, DP, None), P(), P())
    return jax.shard_map(
        on_device, mesh=split, in_specs=placed, out_specs=P(None, TASK), check_vma=False
    )
```

```python
import itertools

import jax
import jax.numpy as jnp
import numpy as np
from jax import lax
from jax.experimental import pallas as pl
from jax.experimental.pallas import tpu as pltpu
from jax.sharding import Mesh
from jax.sharding import PartitionSpec as P

AXES = ("zh", "core", "zl", "y", "x")
SIZES = (4, 2, 2, 4, 4)
DP = ("zl", "y", "x")
TASK = ("zh", "core")
F32, BF16, I16, I32 = jnp.float32, jnp.bfloat16, jnp.int16, jnp.int32

PARTNER = {"a": (1, 0, 3, 2), "b": (3, 2, 1, 0)}
BIT = {"a": (0, 1, 1, 0), "b": (0, 0, 1, 1)}
ORDER = {
    (0, 0): ("xa", "yb", "xb", "ya", "z"),
    (0, 1): ("yb", "xa", "ya", "xb", "z"),
    (1, 0): ("ya", "xb", "xa", "yb", "z"),
    (1, 1): ("xb", "ya", "yb", "xa", "z"),
}
FULL = 32000.0
STEPS = 64.0
EXTRA = 16


def coordinates():
    return [dict(zip(AXES, v)) for v in itertools.product(*map(range, SIZES))]


def linear(co):
    index = 0
    for axis, size in zip(AXES, SIZES):
        index = index * size + co[axis]
    return index


def bit_of(co, dim):
    return co["zl"] if dim == "z" else BIT[dim[1]][co[dim[0]]]


def partner(co, dim):
    if dim == "z":
        return {**co, "zl": 1 - co["zl"]}
    return {**co, dim[0]: PARTNER[dim[1]][co[dim[0]]]}


def swap_along(value, dims):
    pairs = [(linear(co), linear(partner(co, dims[co["core"]]))) for co in coordinates()]
    return lax.ppermute(value, AXES, pairs)


def position(co, core, chunk):
    place = 0
    for dim in ORDER[core, chunk]:
        place = 2 * place + bit_of(co, dim)
    return place


def device_table():
    rows = []
    for co in coordinates():
        core = co["core"]
        row = [core, co["zh"]]
        for chunk in range(2):
            bits = [bit_of(co, dim) for dim in ORDER[core, chunk]]
            row += bits + [0]
        rows.append(row + [0] * (16 - len(row)))
    return np.asarray(rows, np.int32)


def encode(tile):
    top = jnp.maximum(jnp.max(jnp.abs(tile), axis=0, keepdims=True), 1e-30)
    code = jnp.ceil(jnp.log(top) * STEPS)
    values = jnp.round(tile * (jnp.exp(code * (-1.0 / STEPS)) * FULL))
    return values.astype(I32).astype(I16), code


def scales(codes):
    return jnp.exp(codes.astype(I32).astype(F32) * (1.0 / STEPS)) * (1.0 / FULL)


def floats(values):
    return values.astype(I32).astype(F32)


def params(mib=14):
    return pltpu.CompilerParams(vmem_limit_bytes=mib << 20)


def call(kernel, scalars, grid, inputs, in_specs, out_shape, out_specs, scratch, flops, nbytes, **extra):
    return pl.pallas_call(
        kernel,
        out_shape=out_shape,
        grid_spec=pltpu.PrefetchScalarGridSpec(
            num_scalar_prefetch=1,
            grid=grid,
            in_specs=in_specs,
            out_specs=out_specs,
            scratch_shapes=scratch,
        ),
        compiler_params=params(),
        cost_estimate=pl.CostEstimate(flops=flops, bytes_accessed=nbytes, transcendentals=0),
        **extra,
    )(scalars, *inputs)


def whole(shape):
    return pl.BlockSpec(shape, lambda *_: (0,) * len(shape))


ROWS = 512
TILE = 128


def encode_kernel(s_ref, term_ref, out_ref, codes):
    tile = pl.program_id(0)
    values, code = encode(term_ref[...])
    out_ref[pl.ds(pl.multiple_of(tile * TILE, TILE), TILE), :] = values
    codes[pl.ds(tile, 1), :] = code

    @pl.when(tile == ROWS // TILE - 1)
    def _():
        out_ref[ROWS:, :] = codes[...].astype(I32).astype(I16)


def encode_term(table, slot, term):
    rows, width = ROWS, term.shape[1]
    per = rows // TILE
    return call(
        encode_kernel,
        table,
        (per,),
        (term,),
        [pl.BlockSpec((TILE, width), lambda n, s: ((1 - s[slot]) * per + n, 0))],
        jax.ShapeDtypeStruct((rows + EXTRA, width), I16),
        whole((rows + EXTRA, width)),
        [pltpu.VMEM((EXTRA, width), F32)],
        8 * rows * width,
        6 * rows * width,
    )


def term_of(inputs, start, cot):
    part = lax.dynamic_slice(inputs, (0, start), (inputs.shape[0], 2 * ROWS))
    return lax.dot_general(part, cot, (((0,), (0,)), ((), ())), preferred_element_type=F32)


def after(value, *others):
    return lax.optimization_barrier((value, *others))[0]


def level(table, slot, kept, arrived, first=None):
    tasks, rows, width = kept.shape
    rows = rows if first is None else rows // 2
    half = rows // 2
    tile = min(TILE, half)
    per = half // tile
    code_rows = min(TILE, rows)

    def skip(s):
        return 0 if first is None else s[first] * 2 * per

    def kernel(s_ref, keep_ref, give_ref, keep_in, give_in, codes_ref, sum_ref, out_ref, scale, codes):
        task, j = pl.program_id(0), pl.program_id(1)
        bit = s_ref[slot]

        @pl.when((task == 0) & (j == 0))
        def _():
            scale[...] = scales(codes_ref[...])
            codes[...] = jnp.zeros_like(codes)

        def row_of(side):
            return (task * rows + side * half + j * tile) // code_rows

        give = give_ref[0] + floats(give_in[...]) * scale[pl.ds(row_of(1 - bit), 1), :]
        values, code = encode(give)
        at = task * per + j
        out_ref[pl.ds(pl.multiple_of(at * tile, tile), tile), :] = values
        codes[pl.ds(at, 1), :] = code
        sum_ref[0] = keep_ref[0] + floats(keep_in[...]) * scale[pl.ds(row_of(bit), 1), :]

        @pl.when((task == tasks - 1) & (j == per - 1))
        def _():
            out_ref[tasks * half :, :] = codes[...].astype(I32).astype(I16)

    return call(
        kernel,
        table,
        (tasks, per),
        (kept, kept, arrived, arrived, arrived),
        [
            pl.BlockSpec((1, tile, width), lambda t, j, s: (t, skip(s) + s[slot] * per + j, 0)),
            pl.BlockSpec((1, tile, width), lambda t, j, s: (t, skip(s) + (1 - s[slot]) * per + j, 0)),
            pl.BlockSpec((tile, width), lambda t, j, s: ((2 * t + s[slot]) * per + j, 0)),
            pl.BlockSpec((tile, width), lambda t, j, s: ((2 * t + 1 - s[slot]) * per + j, 0)),
            pl.BlockSpec((EXTRA, width), lambda t, j, s: (tasks * rows // EXTRA, 0)),
        ],
        (
            jax.ShapeDtypeStruct((tasks, half, width), F32),
            jax.ShapeDtypeStruct((tasks * half + EXTRA, width), I16),
        ),
        (pl.BlockSpec((1, tile, width), lambda t, j, s: (t, j, 0)), whole((tasks * half + EXTRA, width))),
        [pltpu.VMEM((EXTRA, width), F32), pltpu.VMEM((EXTRA, width), F32)],
        8 * tasks * rows * width,
        tasks * rows * width * 9,
    )


def join_tasks(table, slot, kept, arrived):
    _, rows, width = kept[0].shape
    half = rows // 2

    def kernel(s_ref, keep_a, keep_b, in_a, in_b, sum_ref, out_ref, scale):
        bit = s_ref[slot]
        out_codes = []
        for task, (keep, arr) in enumerate(((keep_a, in_a), (keep_b, in_b))):
            scale[...] = scales(arr[rows:, :])

            def part(side):
                at = pl.ds(pl.multiple_of(side * half, half), half)
                return keep[0, at, :] + floats(arr[at, :]) * scale[pl.ds(side * half // TILE, 1), :]

            values, code = encode(part(1 - bit))
            out_ref[task * half : (task + 1) * half, :] = values
            out_codes.append(code)
            sum_ref[task] = part(bit)
        out_codes.append(jnp.zeros((EXTRA - 2, width), F32))
        out_ref[2 * half :, :] = jnp.concatenate(out_codes, axis=0).astype(I32).astype(I16)

    shapes = ((1, rows, width), (1, rows, width), (rows + EXTRA, width), (rows + EXTRA, width))
    return call(
        kernel,
        table,
        (1,),
        (*kept, *arrived),
        [whole(s) for s in shapes],
        (jax.ShapeDtypeStruct((2, half, width), F32), jax.ShapeDtypeStruct((2 * half + EXTRA, width), I16)),
        (whole((2, half, width)), whole((2 * half + EXTRA, width))),
        [pltpu.VMEM((EXTRA, width), F32)],
        16 * rows * width,
        2 * rows * width * 9,
    )


def line_blocks(kept, arrived):
    _, rows, width = kept[0].shape
    half, wide = rows // 2, width // 4

    def kernel(keep_a, keep_b, in_a, in_b, out_ref, total):
        for chunk, (keep, arr) in enumerate(((keep_a, in_a), (keep_b, in_b))):
            scale = scales(arr[2 * rows :, :])
            for task in range(2):
                values = floats(arr[task * rows : (task + 1) * rows, :])
                total[2 * chunk + task] = keep[task] + values * scale[task : task + 1]
        for side in range(2):
            out_codes = []
            for n in range(4):
                values, code = encode(total[n, side * half : (side + 1) * half, :])
                for zh in range(4):
                    out_ref[2 * zh + side, n * half : (n + 1) * half, :] = values[:, zh * wide : (zh + 1) * wide]
                out_codes.append(code)
            out_codes.append(jnp.zeros((EXTRA - 4, width), F32))
            codes = jnp.concatenate(out_codes, axis=0).astype(I32).astype(I16)
            for zh in range(4):
                out_ref[2 * zh + side, 4 * half :, :] = codes[:, zh * wide : (zh + 1) * wide]

    return pl.pallas_call(
        kernel,
        out_shape=jax.ShapeDtypeStruct((8, 4 * half + EXTRA, wide), I16),
        scratch_shapes=[pltpu.VMEM((4, rows, width), F32)],
        compiler_params=params(),
        cost_estimate=pl.CostEstimate(flops=32 * rows * width, bytes_accessed=36 * rows * width, transcendentals=0),
    )(*kept, *arrived)


def lanes(shape, dim):
    return lax.broadcasted_iota(I32, shape, dim)


def gram_kernel(s_ref, in_ref, grads_ref, gram_ref):
    core = s_ref[0]
    rows = (in_ref.shape[1] - EXTRA) // 4
    for zh in range(4):
        near, far = scales(in_ref[2 * zh, 4 * rows :, :]), scales(in_ref[2 * zh + 1, 4 * rows :, :])
        for n in range(4):
            chunk, task = n // 2, n % 2
            at = slice(n * rows, (n + 1) * rows)
            value = floats(in_ref[2 * zh, at, :]) * near[n : n + 1]
            value = value + floats(in_ref[2 * zh + 1, at, :]) * far[n : n + 1]
            mine = 2 * zh + (task + core - 2 * task * core)
            grads_ref[mine, chunk * rows : (chunk + 1) * rows, :] = value

    grads = [grads_ref[t] for t in range(8)]
    lane, sub = lanes((8, 128), 1), lanes((8, 128), 0)
    matrix = jnp.zeros((8, 128), F32)
    for s in range(8):
        for t in range(s, 8):
            product = grads[s] * grads[t]
            folded = product[:, :128] + product[:, 128:]
            total = jnp.sum(jnp.sum(folded, axis=0, keepdims=True), axis=1, keepdims=True)
            here = ((sub == s) & (lane == t)) | ((sub == t) & (lane == s))
            matrix = jnp.where(here, total, matrix)
    line = jnp.zeros((8, 128), F32)
    for s in range(8):
        row = jnp.where(sub == s, matrix, 0.0)
        line = line + (row if s == 0 else pltpu.roll(row, 8 * s, 1))
    flat = jnp.sum(line, axis=0, keepdims=True)
    gram_ref[...] = jnp.broadcast_to(flat, gram_ref.shape)


def gram(table, arrived):
    _, rows, wide = arrived.shape
    rows = (rows - EXTRA) // 2
    return call(
        gram_kernel,
        table,
        (1,),
        (arrived,),
        [whole(arrived.shape)],
        (jax.ShapeDtypeStruct((8, rows, wide), F32), jax.ShapeDtypeStruct((256, 128), F32)),
        (whole((8, rows, wide)), whole((256, 128))),
        [],
        160 * rows * wide,
        32 * rows * wide,
    )


def combine_kernel(s_ref, order_ref, flags_ref, gram_ref, grads_ref, mine_ref, give_ref):
    core = s_ref[0]
    lane, sub = lanes((8, 128), 1), lanes((8, 128), 0)
    flat = jnp.broadcast_to(jnp.sum(gram_ref[...], axis=0, keepdims=True), (8, 128))
    matrix = jnp.zeros((8, 128), F32)
    for s in range(8):
        row = flat if s == 0 else pltpu.roll(flat, 128 - 8 * s, 1)
        matrix = jnp.where((sub == s) & (lane < 8), row, matrix)
    flags = flags_ref[...].astype(F32)
    small = lanes((8, 8), 1)
    turned = jnp.where(lane == sub, 1.0, 0.0)
    for k in range(8):
        target = order_ref[k]
        column = jnp.sum(jnp.where(lane == target, matrix, 0.0), axis=1, keepdims=True)
        square = jnp.sum(jnp.where(sub[:, :1] == target, column, 0.0), axis=0, keepdims=True)
        active = jnp.sum(jnp.where(small == target, flags, 0.0), axis=1, keepdims=True)
        active = jnp.where(sub[:, :1] == target, 0.0, active)
        active = jnp.sum(jnp.where(lane == sub, active, 0.0), axis=0, keepdims=True)
        dots = jnp.sum(turned * column, axis=0, keepdims=True)
        removed = jnp.minimum(dots, 0.0) / square * active
        turned = turned - jnp.where(sub == target, removed, 0.0)
    weights = jnp.sum(jnp.where(lane < 8, turned, 0.0), axis=1, keepdims=True)
    total = None
    for t in range(8):
        term = weights[t : t + 1] * grads_ref[t]
        total = term if total is None else total + term
    left, right = total[:, :128].astype(BF16), total[:, 128:].astype(BF16)

    @pl.when(core == 0)
    def _():
        mine_ref[...] = left
        give_ref[...] = right

    @pl.when(core == 1)
    def _():
        mine_ref[...] = right
        give_ref[...] = left


def combine(table, order, flags, grams, grads):
    rows = grads.shape[1]
    part = jax.ShapeDtypeStruct((rows, 128), BF16)
    return call(
        combine_kernel,
        table,
        (1,),
        (order, flags, grams, grads),
        [pl.BlockSpec(memory_space=pltpu.SMEM), whole((8, 8)), whole((256, 128)), whole(grads.shape)],
        (part, part),
        (whole((rows, 128)),) * 2,
        [],
        20 * rows * 256,
        40 * rows * 256,
    )


def place_kernel(in_ref, out_ref):
    rows = in_ref.shape[1] // 4
    for n in range(4):

        @pl.when(pl.program_id(0) == n)
        def _():
            for index, (zl, y, x) in enumerate(itertools.product(range(2), range(4), range(4))):
                at = position({"zl": zl, "y": y, "x": x}, n // 2, n % 2) * rows
                out_ref[at : at + rows, :] = in_ref[index, n * rows : (n + 1) * rows, :]


def place(gathered):
    count, rows, cols = gathered.shape
    return pl.pallas_call(
        place_kernel,
        grid=(4,),
        in_specs=[whole(gathered.shape)],
        out_specs=pl.BlockSpec((count * rows // 4, cols), lambda n: (n, 0)),
        out_shape=jax.ShapeDtypeStruct((count * rows, cols), BF16),
        compiler_params=params(),
        cost_estimate=pl.CostEstimate(flops=0, bytes_accessed=4 * count * rows * cols, transcendentals=0),
    )(gathered)


def on_device(inputs, cotangent, task_order, conflict_flags):
    table = jnp.asarray(device_table())[lax.axis_index(AXES)]
    core = lax.axis_index("core")
    own = cotangent[0]
    other = lax.ppermute(own, "core", [(0, 1), (1, 0)])

    dims = [[(ORDER[0, chunk][n], ORDER[1, chunk][n]) for n in range(5)] for chunk in range(2)]
    slots = [2, 8]
    keys = [(task, chunk) for task in range(2) for chunk in range(2)]
    cots = (own, other)
    arrived, kept = {}, {}
    terms = {}
    for task, chunk in keys:
        start = (2 * core + chunk) * 2 * ROWS
        cot = cots[task] if not terms else after(cots[task], coded)
        terms[task, chunk] = term_of(inputs, start, cot)
        coded = encode_term(table, slots[chunk], terms[task, chunk])
        arrived[task, chunk] = swap_along(coded, dims[chunk][0])
    for at in keys:
        chunk = at[1]
        kept[at], coded = level(table, slots[chunk] + 1, terms[at][None], arrived[at], slots[chunk])
        arrived[at] = swap_along(coded, dims[chunk][1])
    joined, taken = [], []
    for chunk in range(2):
        pair = [(task, chunk) for task in range(2)]
        sums = [kept[at] for at in pair]
        if chunk:
            sums[0] = after(sums[0], coded)
        summed, coded = join_tasks(table, slots[chunk] + 2, sums, [arrived[at] for at in pair])
        joined.append(summed)
        taken.append(swap_along(coded, dims[chunk][2]))
    for chunk in range(2):
        if chunk:
            joined[chunk] = after(joined[chunk], coded)
        joined[chunk], coded = level(table, slots[chunk] + 3, joined[chunk], taken[chunk])
        taken[chunk] = swap_along(coded, dims[chunk][3])
    blocks = line_blocks(joined, taken)
    blocks = lax.all_to_all(blocks, ("zh", "zl"), split_axis=0, concat_axis=0, tiled=True)
    grads, grams = gram(table, blocks)
    grams = lax.all_to_all(grams, AXES, split_axis=0, concat_axis=0, tiled=True)
    mine, give = combine(table, task_order, conflict_flags, grams, grads)
    taken = lax.ppermute(give, "core", [(0, 1), (1, 0)])
    first = jnp.where(core == 0, mine, taken)
    second = jnp.where(core == 0, taken, mine)
    block = jnp.concatenate([first, second], axis=0)
    copies = jnp.broadcast_to(block, (32, *block.shape))
    gathered = lax.all_to_all(copies, DP, split_axis=0, concat_axis=0, tiled=True)
    return place(gathered)


def solution(mesh):
    split = Mesh(mesh.devices.reshape(SIZES), AXES)
    placed = (P(DP, None), P(TASK, DP, None), P(), P())
    return jax.shard_map(
        on_device, mesh=split, in_specs=placed, out_specs=P(None, TASK), check_vma=False
    )
```

```python
import itertools

import jax
import jax.numpy as jnp
import numpy as np
from jax import lax
from jax.experimental import pallas as pl
from jax.experimental.pallas import tpu as pltpu
from jax.sharding import Mesh
from jax.sharding import PartitionSpec as P

AXES = ("zh", "core", "zl", "y", "x")
SIZES = (4, 2, 2, 4, 4)
DP = ("zl", "y", "x")
TASK = ("zh", "core")
F32, BF16, I16, I32 = jnp.float32, jnp.bfloat16, jnp.int16, jnp.int32

PARTNER = {"a": (1, 0, 3, 2), "b": (3, 2, 1, 0)}
BIT = {"a": (0, 1, 1, 0), "b": (0, 0, 1, 1)}
ORDER = {
    (0, 0): ("xa", "yb", "xb", "ya", "z"),
    (0, 1): ("yb", "xa", "ya", "xb", "z"),
    (1, 0): ("ya", "xb", "xa", "yb", "z"),
    (1, 1): ("xb", "ya", "yb", "xa", "z"),
}
FULL = 32000.0
STEPS = 64.0
EXTRA = 16


def coordinates():
    return [dict(zip(AXES, v)) for v in itertools.product(*map(range, SIZES))]


def linear(co):
    index = 0
    for axis, size in zip(AXES, SIZES):
        index = index * size + co[axis]
    return index


def bit_of(co, dim):
    return co["zl"] if dim == "z" else BIT[dim[1]][co[dim[0]]]


def partner(co, dim):
    if dim == "z":
        return {**co, "zl": 1 - co["zl"]}
    return {**co, dim[0]: PARTNER[dim[1]][co[dim[0]]]}


def swap_along(value, dims):
    pairs = [(linear(co), linear(partner(co, dims[co["core"]]))) for co in coordinates()]
    return lax.ppermute(value, AXES, pairs)


def position(co, core, chunk):
    place = 0
    for dim in ORDER[core, chunk]:
        place = 2 * place + bit_of(co, dim)
    return place


def device_table():
    rows = []
    for co in coordinates():
        core = co["core"]
        row = [core, co["zh"]]
        for chunk in range(2):
            bits = [bit_of(co, dim) for dim in ORDER[core, chunk]]
            row += bits + [0]
        rows.append(row + [0] * (16 - len(row)))
    return np.asarray(rows, np.int32)


def encode(tile):
    top = jnp.maximum(jnp.max(jnp.abs(tile), axis=0, keepdims=True), 1e-30)
    code = jnp.ceil(jnp.log(top) * STEPS)
    values = jnp.round(tile * (jnp.exp(code * (-1.0 / STEPS)) * FULL))
    return values.astype(I32).astype(I16), code


def scales(codes):
    return jnp.exp(codes.astype(I32).astype(F32) * (1.0 / STEPS)) * (1.0 / FULL)


def floats(values):
    return values.astype(I32).astype(F32)


def params(mib=14):
    return pltpu.CompilerParams(vmem_limit_bytes=mib << 20)


def call(kernel, scalars, grid, inputs, in_specs, out_shape, out_specs, scratch, flops, nbytes, **extra):
    return pl.pallas_call(
        kernel,
        out_shape=out_shape,
        grid_spec=pltpu.PrefetchScalarGridSpec(
            num_scalar_prefetch=1,
            grid=grid,
            in_specs=in_specs,
            out_specs=out_specs,
            scratch_shapes=scratch,
        ),
        compiler_params=params(),
        cost_estimate=pl.CostEstimate(flops=flops, bytes_accessed=nbytes, transcendentals=0),
        **extra,
    )(scalars, *inputs)


def whole(shape):
    return pl.BlockSpec(shape, lambda *_: (0,) * len(shape))


ROWS = 512
TILE = 128


def encode_kernel(s_ref, term_ref, out_ref, codes):
    tile = pl.program_id(0)
    values, code = encode(term_ref[...])
    out_ref[pl.ds(pl.multiple_of(tile * TILE, TILE), TILE), :] = values
    codes[pl.ds(tile, 1), :] = code

    @pl.when(tile == ROWS // TILE - 1)
    def _():
        out_ref[ROWS:, :] = codes[...].astype(I32).astype(I16)


def encode_term(table, slot, term):
    rows, width = ROWS, term.shape[1]
    per = rows // TILE
    return call(
        encode_kernel,
        table,
        (per,),
        (term,),
        [pl.BlockSpec((TILE, width), lambda n, s: ((1 - s[slot]) * per + n, 0))],
        jax.ShapeDtypeStruct((rows + EXTRA, width), I16),
        whole((rows + EXTRA, width)),
        [pltpu.VMEM((EXTRA, width), F32)],
        8 * rows * width,
        6 * rows * width,
    )


def term_of(inputs, start, cot):
    part = lax.dynamic_slice(inputs, (0, start), (inputs.shape[0], 2 * ROWS))
    return lax.dot_general(part, cot, (((0,), (0,)), ((), ())), preferred_element_type=F32)


def after(value, *others):
    return lax.optimization_barrier((value, *others))[0]


def level(table, slot, kept, arrived, first=None):
    tasks, rows, width = kept.shape
    rows = rows if first is None else rows // 2
    half = rows // 2
    tile = min(TILE, half)
    per = half // tile
    code_rows = min(TILE, rows)

    def skip(s):
        return 0 if first is None else s[first] * 2 * per

    def kernel(s_ref, keep_ref, give_ref, keep_in, give_in, codes_ref, sum_ref, out_ref, scale, codes):
        task, j = pl.program_id(0), pl.program_id(1)
        bit = s_ref[slot]

        @pl.when((task == 0) & (j == 0))
        def _():
            scale[...] = scales(codes_ref[...])
            codes[...] = jnp.zeros_like(codes)

        def row_of(side):
            return (task * rows + side * half + j * tile) // code_rows

        give = give_ref[0] + floats(give_in[...]) * scale[pl.ds(row_of(1 - bit), 1), :]
        values, code = encode(give)
        at = task * per + j
        out_ref[pl.ds(pl.multiple_of(at * tile, tile), tile), :] = values
        codes[pl.ds(at, 1), :] = code
        sum_ref[0] = keep_ref[0] + floats(keep_in[...]) * scale[pl.ds(row_of(bit), 1), :]

        @pl.when((task == tasks - 1) & (j == per - 1))
        def _():
            out_ref[tasks * half :, :] = codes[...].astype(I32).astype(I16)

    return call(
        kernel,
        table,
        (tasks, per),
        (kept, kept, arrived, arrived, arrived),
        [
            pl.BlockSpec((1, tile, width), lambda t, j, s: (t, skip(s) + s[slot] * per + j, 0)),
            pl.BlockSpec((1, tile, width), lambda t, j, s: (t, skip(s) + (1 - s[slot]) * per + j, 0)),
            pl.BlockSpec((tile, width), lambda t, j, s: ((2 * t + s[slot]) * per + j, 0)),
            pl.BlockSpec((tile, width), lambda t, j, s: ((2 * t + 1 - s[slot]) * per + j, 0)),
            pl.BlockSpec((EXTRA, width), lambda t, j, s: (tasks * rows // EXTRA, 0)),
        ],
        (
            jax.ShapeDtypeStruct((tasks, half, width), F32),
            jax.ShapeDtypeStruct((tasks * half + EXTRA, width), I16),
        ),
        (pl.BlockSpec((1, tile, width), lambda t, j, s: (t, j, 0)), whole((tasks * half + EXTRA, width))),
        [pltpu.VMEM((EXTRA, width), F32), pltpu.VMEM((EXTRA, width), F32)],
        8 * tasks * rows * width,
        tasks * rows * width * 9,
    )


def join_tasks(table, slot, kept, arrived):
    _, rows, width = kept[0].shape
    half = rows // 2

    def kernel(s_ref, keep_a, keep_b, in_a, in_b, sum_ref, out_ref, scale):
        bit = s_ref[slot]
        out_codes = []
        for task, (keep, arr) in enumerate(((keep_a, in_a), (keep_b, in_b))):
            scale[...] = scales(arr[rows:, :])

            def part(side):
                at = pl.ds(pl.multiple_of(side * half, half), half)
                return keep[0, at, :] + floats(arr[at, :]) * scale[pl.ds(side * half // TILE, 1), :]

            values, code = encode(part(1 - bit))
            out_ref[task * half : (task + 1) * half, :] = values
            out_codes.append(code)
            sum_ref[task] = part(bit)
        out_codes.append(jnp.zeros((EXTRA - 2, width), F32))
        out_ref[2 * half :, :] = jnp.concatenate(out_codes, axis=0).astype(I32).astype(I16)

    shapes = ((1, rows, width), (1, rows, width), (rows + EXTRA, width), (rows + EXTRA, width))
    return call(
        kernel,
        table,
        (1,),
        (*kept, *arrived),
        [whole(s) for s in shapes],
        (jax.ShapeDtypeStruct((2, half, width), F32), jax.ShapeDtypeStruct((2 * half + EXTRA, width), I16)),
        (whole((2, half, width)), whole((2 * half + EXTRA, width))),
        [pltpu.VMEM((EXTRA, width), F32)],
        16 * rows * width,
        2 * rows * width * 9,
    )


def line_blocks(kept, arrived):
    _, rows, width = kept[0].shape
    half, wide = rows // 2, width // 4

    def kernel(keep_a, keep_b, in_a, in_b, out_ref, total):
        for chunk, (keep, arr) in enumerate(((keep_a, in_a), (keep_b, in_b))):
            scale = scales(arr[2 * rows :, :])
            for task in range(2):
                values = floats(arr[task * rows : (task + 1) * rows, :])
                total[2 * chunk + task] = keep[task] + values * scale[task : task + 1]
        for side in range(2):
            out_codes = []
            for n in range(4):
                values, code = encode(total[n, side * half : (side + 1) * half, :])
                for zh in range(4):
                    out_ref[2 * zh + side, n * half : (n + 1) * half, :] = values[:, zh * wide : (zh + 1) * wide]
                out_codes.append(code)
            out_codes.append(jnp.zeros((EXTRA - 4, width), F32))
            codes = jnp.concatenate(out_codes, axis=0).astype(I32).astype(I16)
            for zh in range(4):
                out_ref[2 * zh + side, 4 * half :, :] = codes[:, zh * wide : (zh + 1) * wide]

    return pl.pallas_call(
        kernel,
        out_shape=jax.ShapeDtypeStruct((8, 4 * half + EXTRA, wide), I16),
        scratch_shapes=[pltpu.VMEM((4, rows, width), F32)],
        compiler_params=params(),
        cost_estimate=pl.CostEstimate(flops=32 * rows * width, bytes_accessed=36 * rows * width, transcendentals=0),
    )(*kept, *arrived)


def lanes(shape, dim):
    return lax.broadcasted_iota(I32, shape, dim)


def gram_kernel(s_ref, in_ref, grads_ref, gram_ref):
    core = s_ref[0]
    rows = (in_ref.shape[1] - EXTRA) // 4
    for zh in range(4):
        near, far = scales(in_ref[2 * zh, 4 * rows :, :]), scales(in_ref[2 * zh + 1, 4 * rows :, :])
        for n in range(4):
            chunk, task = n // 2, n % 2
            at = slice(n * rows, (n + 1) * rows)
            value = floats(in_ref[2 * zh, at, :]) * near[n : n + 1]
            value = value + floats(in_ref[2 * zh + 1, at, :]) * far[n : n + 1]
            mine = 2 * zh + (task + core - 2 * task * core)
            grads_ref[mine, chunk * rows : (chunk + 1) * rows, :] = value

    grads = [grads_ref[t] for t in range(8)]
    lane, sub = lanes((8, 128), 1), lanes((8, 128), 0)
    matrix = jnp.zeros((8, 128), F32)
    for s in range(8):
        for t in range(s, 8):
            product = grads[s] * grads[t]
            folded = product[:, :128] + product[:, 128:]
            total = jnp.sum(jnp.sum(folded, axis=0, keepdims=True), axis=1, keepdims=True)
            here = ((sub == s) & (lane == t)) | ((sub == t) & (lane == s))
            matrix = jnp.where(here, total, matrix)
    line = jnp.zeros((8, 128), F32)
    for s in range(8):
        row = jnp.where(sub == s, matrix, 0.0)
        line = line + (row if s == 0 else pltpu.roll(row, 8 * s, 1))
    flat = jnp.sum(line, axis=0, keepdims=True)
    gram_ref[...] = jnp.broadcast_to(flat, gram_ref.shape)


def gram(table, arrived):
    _, rows, wide = arrived.shape
    rows = (rows - EXTRA) // 2
    return call(
        gram_kernel,
        table,
        (1,),
        (arrived,),
        [whole(arrived.shape)],
        (jax.ShapeDtypeStruct((8, rows, wide), F32), jax.ShapeDtypeStruct((256, 128), F32)),
        (whole((8, rows, wide)), whole((256, 128))),
        [],
        160 * rows * wide,
        32 * rows * wide,
    )


def combine_kernel(s_ref, order_ref, flags_ref, gram_ref, grads_ref, mine_ref, give_ref):
    core = s_ref[0]
    lane, sub = lanes((8, 128), 1), lanes((8, 128), 0)
    flat = jnp.broadcast_to(jnp.sum(gram_ref[...], axis=0, keepdims=True), (8, 128))
    matrix = jnp.zeros((8, 128), F32)
    for s in range(8):
        row = flat if s == 0 else pltpu.roll(flat, 128 - 8 * s, 1)
        matrix = jnp.where((sub == s) & (lane < 8), row, matrix)
    flags = flags_ref[...].astype(F32)
    small = lanes((8, 8), 1)
    turned = jnp.where(lane == sub, 1.0, 0.0)
    for k in range(8):
        target = order_ref[k]
        column = jnp.sum(jnp.where(lane == target, matrix, 0.0), axis=1, keepdims=True)
        square = jnp.sum(jnp.where(sub[:, :1] == target, column, 0.0), axis=0, keepdims=True)
        active = jnp.sum(jnp.where(small == target, flags, 0.0), axis=1, keepdims=True)
        active = jnp.where(sub[:, :1] == target, 0.0, active)
        active = jnp.sum(jnp.where(lane == sub, active, 0.0), axis=0, keepdims=True)
        dots = jnp.sum(turned * column, axis=0, keepdims=True)
        removed = jnp.minimum(dots, 0.0) / square * active
        turned = turned - jnp.where(sub == target, removed, 0.0)
    weights = jnp.sum(jnp.where(lane < 8, turned, 0.0), axis=1, keepdims=True)
    total = None
    for t in range(8):
        term = weights[t : t + 1] * grads_ref[t]
        total = term if total is None else total + term
    left, right = total[:, :128].astype(BF16), total[:, 128:].astype(BF16)

    @pl.when(core == 0)
    def _():
        mine_ref[...] = left
        give_ref[...] = right

    @pl.when(core == 1)
    def _():
        mine_ref[...] = right
        give_ref[...] = left


def combine(table, order, flags, grams, grads):
    rows = grads.shape[1]
    part = jax.ShapeDtypeStruct((rows, 128), BF16)
    return call(
        combine_kernel,
        table,
        (1,),
        (order, flags, grams, grads),
        [pl.BlockSpec(memory_space=pltpu.SMEM), whole((8, 8)), whole((256, 128)), whole(grads.shape)],
        (part, part),
        (whole((rows, 128)),) * 2,
        [],
        20 * rows * 256,
        40 * rows * 256,
    )


def place_kernel(in_ref, out_ref):
    rows = in_ref.shape[1] // 4
    for index, (zl, y, x) in enumerate(itertools.product(range(2), range(4), range(4))):
        co = {"zl": zl, "y": y, "x": x}
        for n in range(4):
            at = (n * 32 + position(co, n // 2, n % 2)) * rows
            out_ref[at : at + rows, :] = in_ref[index, n * rows : (n + 1) * rows, :]


def place(gathered):
    count, rows, cols = gathered.shape
    return pl.pallas_call(
        place_kernel,
        out_shape=jax.ShapeDtypeStruct((count * rows, cols), BF16),
        compiler_params=params(),
        cost_estimate=pl.CostEstimate(flops=0, bytes_accessed=4 * count * rows * cols, transcendentals=0),
    )(gathered)


def on_device(inputs, cotangent, task_order, conflict_flags):
    table = jnp.asarray(device_table())[lax.axis_index(AXES)]
    core = lax.axis_index("core")
    own = cotangent[0]
    other = lax.ppermute(own, "core", [(0, 1), (1, 0)])

    dims = [[(ORDER[0, chunk][n], ORDER[1, chunk][n]) for n in range(5)] for chunk in range(2)]
    slots = [2, 8]
    keys = [(task, chunk) for task in range(2) for chunk in range(2)]
    cots = (own, other)
    arrived, kept = {}, {}
    terms = {}
    for task, chunk in keys:
        start = (2 * core + chunk) * 2 * ROWS
        cot = cots[task] if not terms else after(cots[task], coded)
        terms[task, chunk] = term_of(inputs, start, cot)
        coded = encode_term(table, slots[chunk], terms[task, chunk])
        arrived[task, chunk] = swap_along(coded, dims[chunk][0])
    for at in keys:
        chunk = at[1]
        term = terms[at][None]
        if at != keys[0]:
            term = after(term, coded)
        kept[at], coded = level(table, slots[chunk] + 1, term, arrived[at], slots[chunk])
        arrived[at] = swap_along(coded, dims[chunk][1])
    joined, taken = {}, {}
    coded = arrived[keys[0]]
    for chunk in (1, 0):
        pair = [(task, chunk) for task in range(2)]
        sums = [kept[at] for at in pair]
        sums[0] = after(sums[0], coded)
        joined[chunk], coded = join_tasks(table, slots[chunk] + 2, sums, [arrived[at] for at in pair])
        taken[chunk] = swap_along(coded, dims[chunk][2])
    for chunk in (1, 0):
        if chunk == 0:
            joined[chunk] = after(joined[chunk], coded)
        joined[chunk], coded = level(table, slots[chunk] + 3, joined[chunk], taken[chunk])
        taken[chunk] = swap_along(coded, dims[chunk][3])
    blocks = line_blocks([joined[0], joined[1]], [taken[0], taken[1]])
    blocks = lax.all_to_all(blocks, ("zh", "zl"), split_axis=0, concat_axis=0, tiled=True)
    grads, grams = gram(table, blocks)
    grams = lax.all_to_all(grams, AXES, split_axis=0, concat_axis=0, tiled=True)
    mine, give = combine(table, task_order, conflict_flags, grams, grads)
    taken = lax.ppermute(give, "core", [(0, 1), (1, 0)])
    first = jnp.where(core == 0, mine, taken)
    second = jnp.where(core == 0, taken, mine)
    block = jnp.concatenate([first, second], axis=0)
    copies = jnp.broadcast_to(block, (32, *block.shape))
    gathered = lax.all_to_all(copies, DP, split_axis=0, concat_axis=0, tiled=True)
    return place(gathered)


def solution(mesh):
    split = Mesh(mesh.devices.reshape(SIZES), AXES)
    placed = (P(DP, None), P(TASK, DP, None), P(), P())
    return jax.shard_map(
        on_device, mesh=split, in_specs=placed, out_specs=P(None, TASK), check_vma=False
    )
```
